128 devices in a mesh: pp: 2 (over core), ep: 16 (over y, x), dp: 4 (over z).
Axes of the slice: x: 4, y: 4, z: 4, core: 2. Of those that a mesh axis runs over, the one named last changes fastest.
Arguments:
- tokens: bfloat16 [4096, 3072], P('ep'), may hold values from -6 to 6
- norm_gain: float32 [3072], replicated, may hold values from 0.25 to 1.75
- router_weight: bfloat16 [3072, 16], replicated, may hold values from -0.109375 to 0.109375
- expert_ids: int32 [4096, 4], P('ep'), may hold values from 0 to 15, all different within a row; in each aligned block of 256 rows (0 to 255, 256 to 511, ...) at most 72 rows name the same one
- up_weight: bfloat16 [16, 3072, 6144], P('ep', None, ('pp', 'dp')), may hold values from -0.109375 to 0.109375
- down_weight: bfloat16 [16, 6144, 3072], P('ep', ('pp', 'dp')), may hold values from -0.078125 to 0.078125
Outputs:
- mixed: bfloat16 [4096, 3072], P('ep')
The draws below stay inside these ranges and needn't reach their ends.
Inputs may be any that keep to these rules, and one draw needn't show every extreme that they name: `expert_ids`: each row names 4 different experts. In each aligned block of 256 rows (the rows of one index of ep) no expert is named by more than 72 rows, a bound that some block reaches.
All inputs are finite; a program needn't handle non-finite values.
Results may differ from the reference program's by a relative error of at most 0.0085.
Values may be sent and summed in bfloat16 or wider, within the bound.
No kernel may reach another device: no remote copies, remote signals or barrier semaphores. Data moves between devices by JAX's collectives and lax.ppermute only.
A program may use at most 576 MiB of HBM per device.

```python
import math
import jax
import jax.numpy as jnp
import numpy as np
from jax import lax

D = 3072
EXPERTS = 16
TOP = 4
FF = 6144
TOK_DEV = 256
CAP = 72
TOKENS = 4096


def levels(rng, shape, cuts, low, high):
    loudness = 1.0
    for dim, parts in cuts:
        heights = jax.random.uniform(jax.random.fold_in(jax.random.fold_in(rng, 6), dim), (parts,), jnp.float32, low / len(cuts), high / len(cuts))
        loudness = loudness * jnp.repeat(jnp.exp(heights), shape[dim] // parts).reshape((-1,) + (1,) * (len(shape) - 1 - dim))
    return loudness


def deal_out(rng, own, number, rows, amount, top, most, lean):
    ranking = jax.random.permutation(rng, amount)
    heavy_load, common = load_shares(amount, rows * top, most, lean, True), load_shares(amount, rows * top, most, lean, False)
    places = jnp.arange(amount)

    def named(tallies, turn):
        used = int((tallies > 0).sum())
        fixed = max(1, used // 4)
        moved = fixed + (places - fixed + turn * (used - fixed)) % max(1, amount - fixed)
        return jnp.zeros((amount,), jnp.int32).at[ranking[jnp.where(places < fixed, places, moved)]].set(jnp.asarray(tallies, jnp.int32))

    tallies = jnp.where(number % 4 == 0, named(heavy_load, number // 4), named(common, number - number // 4 - 1))
    mixed = jax.random.permutation(jax.random.fold_in(own, 3), amount)
    donor, receiver = mixed[0:amount // 2 * 2:2], mixed[1:amount // 2 * 2:2]
    slack = jnp.minimum(tallies[donor] - 1, most - tallies[receiver]) // 2
    slack = jnp.where((donor == ranking[0]) | (receiver == ranking[0]) | (tallies[receiver] == 0), 0, jnp.maximum(slack, 0))
    moved = jax.random.randint(jax.random.fold_in(own, 4), (amount // 2,), 0, 1 << 20) % (slack + 1)
    tallies = tallies.at[donor].add(-moved).at[receiver].add(moved)
    members = jnp.searchsorted(jnp.cumsum(tallies), jnp.arange(rows * top), side="right").astype(jnp.int32)
    table = members.reshape(top, rows).T
    table = table[jax.random.permutation(jax.random.fold_in(own, 1), rows)]
    turn = jax.random.randint(jax.random.fold_in(own, 2), (rows, 1), 0, top)
    return jnp.take_along_axis(table, (jnp.arange(top)[None, :] + turn) % top, axis=1)


def load_shares(number_of, total, limit, slope, full):
    portions = [(1 << 20) // math.isqrt(standing ** slope) + 1 for standing in range(1, number_of + 1)]
    largest = limit if full else min(limit, max(-(-total // number_of), total * portions[0] // sum(portions)))
    least = 1 if total - largest >= number_of - 1 else 0
    given, spare = [largest] + [least] * (number_of - 1), total - largest - least * (number_of - 1)
    while spare > 0:
        movable = [i for i in range(1, number_of) if given[i] < largest] or [i for i in range(1, number_of) if given[i] < limit]
        pool, left = sum([portions[i] for i in movable]), spare
        for i in movable:
            more = min(limit - given[i], max(1, left * portions[i] // pool), spare)
            given[i] = given[i] + more
            spare = spare - more
    return np.array(given)


def bell_draw(own_key, shape, scale, most, cuts=(), held_as=jnp.bfloat16):
    gain = levels(own_key, shape, cuts, -0.22, 0.18) if cuts else 1.0
    values = jax.random.normal(own_key, shape, jnp.float32) * scale * gain
    return jnp.minimum(jnp.maximum(values, -most), most).astype(held_as)


def setup_inputs(seed: int = 0) -> dict:
    keys = jax.random.split(jax.random.key(seed), 7)
    tokens = bell_draw(keys[0], (TOKENS, D), 1.0, 6.0, ((0, 16),))
    norm_gain = jnp.clip(1.0 + 0.15 * jax.random.normal(keys[1], (D,), jnp.float32), 0.25, 1.75)
    router_weight = bell_draw(keys[2], (D, EXPERTS), D ** -0.5, 0.109375)
    expert_ids_keys = jax.random.split(jax.random.fold_in(keys[3], 1), TOKENS // TOK_DEV)
    expert_ids_turns = jax.random.permutation(jax.random.fold_in(keys[3], 3), TOKENS // TOK_DEV)
    expert_ids = jax.vmap(lambda own, number: deal_out(jax.random.fold_in(keys[3], 2), own, number, TOK_DEV, EXPERTS, TOP, CAP, 1))(expert_ids_keys, expert_ids_turns).reshape((TOKENS, TOP))
    up_weight = bell_draw(keys[4], (EXPERTS, D, FF), D ** -0.5, 0.109375, ((0, 16), (2, 8)))
    down_weight = bell_draw(keys[5], (EXPERTS, FF, D), FF ** -0.5, 0.078125, ((0, 16), (1, 8)))
    return dict(tokens=tokens, norm_gain=norm_gain, router_weight=router_weight, expert_ids=expert_ids, up_weight=up_weight, down_weight=down_weight)


EPSILON = 1e-05

def layer_norm(values_in, gain_row):
    values = values_in.astype(jnp.float32)
    center = lax.optimization_barrier(jnp.mean(values, axis=-1, keepdims=True))
    shifted = values - center
    spread = lax.optimization_barrier(jnp.mean(shifted * shifted, axis=-1, keepdims=True))
    return (shifted / jnp.sqrt(spread + EPSILON) * gain_row).astype(jnp.bfloat16)

def expert_block(slab_rows, up_matrix, down_matrix):
    up_proj = jnp.dot(slab_rows, up_matrix, preferred_element_type=jnp.float32)
    active = jax.nn.silu(up_proj).astype(jnp.bfloat16)
    return jnp.dot(active, down_matrix, preferred_element_type=jnp.float32).astype(jnp.bfloat16)

def reference(tokens, norm_gain, router_weight, expert_ids, up_weight, down_weight):
    normed = layer_norm(tokens, norm_gain)
    logits = jnp.dot(normed, router_weight, preferred_element_type=jnp.float32)
    weight = jnp.exp(jnp.take_along_axis(logits, expert_ids, axis=1))
    gate_values = weight / lax.optimization_barrier(jnp.sum(weight, axis=1, keepdims=True))
    blocks = TOKENS // TOK_DEV
    flat_ids = expert_ids.reshape(blocks, TOK_DEV * TOP)
    onehot = (flat_ids[:, :, None] == jnp.arange(EXPERTS, dtype=jnp.int32)[None, None, :]).astype(jnp.int32)
    before = jnp.cumsum(onehot, axis=1) - onehot
    position = lax.optimization_barrier(jnp.sum(before * onehot, axis=2))
    slot_index = (flat_ids * CAP + position).astype(jnp.int32)
    token_rows = jnp.repeat(normed.reshape(blocks, TOK_DEV, D), TOP, axis=1)
    block_index = jnp.broadcast_to(jnp.arange(blocks, dtype=jnp.int32)[:, None], slot_index.shape)
    buffer = jnp.zeros((blocks, EXPERTS * CAP, D), jnp.bfloat16).at[block_index, slot_index].set(token_rows)
    per_expert = jnp.transpose(buffer.reshape(blocks, EXPERTS, CAP, D), (1, 0, 2, 3)).reshape(EXPERTS, blocks * CAP, D)

    def run_expert(expert_item):
        return expert_block(expert_item[0], expert_item[1], expert_item[2])
    expert_out = lax.map(run_expert, (per_expert, up_weight, down_weight))
    expert_out = jnp.transpose(expert_out.reshape(EXPERTS, blocks, CAP, D), (1, 0, 2, 3)).reshape(blocks, EXPERTS * CAP, D)
    outputs = expert_out[block_index, slot_index].reshape(-1, TOP, D)
    mixed_out = lax.optimization_barrier(jnp.sum(gate_values[:, :, None] * outputs.astype(jnp.float32), axis=1))
    return (tokens.astype(jnp.float32) + mixed_out).astype(jnp.bfloat16)
```

```python
import jax
import jax.numpy as jnp
from jax import lax
from jax.experimental import pallas as pl
from jax.experimental.pallas import tpu as pltpu
from jax.sharding import PartitionSpec as P

D = 3072
EXPERTS = 16
TOP = 4
TOK_DEV = 256
CAP = 72
ROWS = EXPERTS * CAP
HALF = D // 2
SHARE = D // 8
EPSILON = 1e-05
F32 = jnp.float32
BF16 = jnp.bfloat16
VMEM_LIMIT = 60 * 1024 * 1024
NT = (((1,), (1,)), ((), ()))


def route_kernel(tok_ref, gain_ref, router_ref, ids_ref, buf_ref, mix_ref, normed_ref, key_ref):
    step = pl.program_id(0)
    experts_a_step = EXPERTS // pl.num_programs(0)

    @pl.when(step == 0)
    def _():
        def norm_rows(part, carry):
            rows = pl.ds(pl.multiple_of(part * 32, 32), 32)
            values = tok_ref[rows, :].astype(F32)
            shifted = values - jnp.mean(values, axis=-1, keepdims=True)
            spread = jnp.mean(shifted * shifted, axis=-1, keepdims=True)
            normed = (shifted * lax.rsqrt(spread + EPSILON) * gain_ref[...]).astype(BF16)
            normed_ref[0, rows, :] = normed[:, :HALF]
            normed_ref[1, rows, :] = normed[:, HALF:]
            return carry

        lax.fori_loop(0, TOK_DEV // 32, norm_rows, 0)
        logits = lax.dot_general(normed_ref[0], router_ref[:, :HALF], NT, preferred_element_type=F32)
        logits += lax.dot_general(normed_ref[1], router_ref[:, HALF:], NT, preferred_element_type=F32)

        named = jnp.zeros((EXPERTS, TOK_DEV), jnp.int32)
        expert = lax.broadcasted_iota(jnp.int32, (EXPERTS, TOK_DEV), 0)
        for k in range(TOP):
            named += (ids_ref[k : k + 1, :] == expert).astype(jnp.int32)
        named = named.astype(F32)
        row = lax.broadcasted_iota(jnp.int32, (TOK_DEV, TOK_DEV), 0)
        col = lax.broadcasted_iota(jnp.int32, (TOK_DEV, TOK_DEV), 1)
        earlier = (row > col).astype(F32).astype(BF16)
        same = (row == col).astype(F32).astype(BF16)
        named_bf = named.astype(BF16)
        place_t = lax.dot_general(named_bf, earlier, NT, preferred_element_type=F32)
        key_ref[...] = jnp.where(named > 0.5, place_t, -1.0)
        place = lax.dot_general(earlier, named_bf, NT, preferred_element_type=F32)
        chosen = lax.dot_general(same, named_bf, NT, preferred_element_type=F32) > 0.5
        key = jnp.where(chosen, place, -1.0)
        weight = jnp.where(chosen, jnp.exp(logits), 0.0)
        gate = weight / jnp.sum(weight, axis=1, keepdims=True)

        slot = lax.broadcasted_iota(jnp.int32, (EXPERTS, ROWS), 1)
        first = lax.broadcasted_iota(jnp.int32, (EXPERTS, ROWS), 0) * CAP
        inside = (slot >= first) & (slot < first + CAP)
        spread_out = inside.astype(F32).astype(BF16)
        slot_in = jnp.sum(jnp.where(inside, slot - first, 0).astype(F32), axis=0, keepdims=True)
        key_wide = jnp.dot(key.astype(BF16), spread_out, preferred_element_type=F32)
        gate_wide = jnp.dot(gate.astype(BF16), spread_out, preferred_element_type=F32)
        mix_ref[...] = jnp.where(key_wide == slot_in, gate_wide, 0.0).astype(BF16)

    keys = key_ref[pl.ds(pl.multiple_of(step * experts_a_step, experts_a_step), experts_a_step), :]
    slot_row = lax.broadcasted_iota(jnp.int32, (CAP, TOK_DEV), 0).astype(F32)
    picks = [(slot_row == keys[e : e + 1, :]).astype(F32) for e in range(experts_a_step)]
    pick = jnp.concatenate(picks, axis=0).astype(BF16)
    buf_ref[...] = jnp.dot(pick, normed_ref[lax.axis_index("pp")], preferred_element_type=F32).astype(BF16)


def route(tokens, norm_gain, router_weight, expert_ids):
    steps = 2
    whole = lambda i: (0, 0)
    return pl.pallas_call(
        route_kernel,
        grid=(steps,),
        in_specs=[
            pl.BlockSpec((TOK_DEV, D), whole),
            pl.BlockSpec((1, D), whole),
            pl.BlockSpec((EXPERTS, D), whole),
            pl.BlockSpec((TOP, TOK_DEV), whole),
        ],
        out_specs=[
            pl.BlockSpec((ROWS // steps, HALF), lambda i: (i, 0)),
            pl.BlockSpec((TOK_DEV, ROWS), whole),
        ],
        out_shape=[
            jax.ShapeDtypeStruct((ROWS, HALF), BF16),
            jax.ShapeDtypeStruct((TOK_DEV, ROWS), BF16),
        ],
        scratch_shapes=[
            pltpu.VMEM((2, TOK_DEV, HALF), BF16),
            pltpu.VMEM((EXPERTS, TOK_DEV), F32),
        ],
        compiler_params=pltpu.CompilerParams(vmem_limit_bytes=VMEM_LIMIT),
        cost_estimate=pl.CostEstimate(flops=2 * ROWS * TOK_DEV * HALF, bytes_accessed=6_000_000, transcendentals=0),
    )(tokens, norm_gain.reshape(1, D), router_weight.T, expert_ids.T)


def up_first_kernel(at_ref, x_ref, w_ref, out_ref):
    out_ref[...] = jnp.dot(x_ref[...], w_ref[0], preferred_element_type=F32)


def up_second_kernel(at_ref, x_ref, w_ref, part_ref, out_ref):
    value = part_ref[...] + jnp.dot(x_ref[...], w_ref[0], preferred_element_type=F32)
    out_ref[...] = (value / (1.0 + jnp.exp(-value))).astype(BF16)


def up_half(at, rows_in, weight, part=None):
    count, inner = rows_in.shape
    units = weight.shape[2]
    block = count // 4
    row_block = lambda i, at: (i, 0)
    specs = [pl.BlockSpec((block, inner), row_block), pl.BlockSpec((1, inner, units), lambda i, at: (at[0], 0, 0))]
    args = [rows_in, weight]
    if part is not None:
        specs.append(pl.BlockSpec((block, units), row_block))
        args.append(part)
    return pl.pallas_call(
        up_first_kernel if part is None else up_second_kernel,
        grid_spec=pltpu.PrefetchScalarGridSpec(
            num_scalar_prefetch=1,
            grid=(4,),
            in_specs=specs,
            out_specs=pl.BlockSpec((block, units), row_block),
        ),
        out_shape=jax.ShapeDtypeStruct((count, units), F32 if part is None else BF16),
        compiler_params=pltpu.CompilerParams(vmem_limit_bytes=VMEM_LIMIT),
        cost_estimate=pl.CostEstimate(flops=2 * count * inner * units, bytes_accessed=9_000_000, transcendentals=0),
    )(at, *args)


def down_first_kernel(at_ref, h_ref, w_ref, out_ref):
    out_ref[0] = jnp.dot(h_ref[...], w_ref[...], preferred_element_type=F32).astype(BF16)


def down_second_kernel(at_ref, h_ref, w_ref, got_ref, out_ref):
    value = jnp.dot(h_ref[...], w_ref[...], preferred_element_type=F32)
    out_ref[0] = (value + got_ref[0].astype(F32)).astype(BF16)


def down_half(at, hidden, weight, got=None):
    count, units = hidden.shape
    piece = lambda i, at: (i, 0, 0)
    specs = [
        pl.BlockSpec((count, units), lambda i, at: (0, 0)),
        pl.BlockSpec((units, SHARE), lambda i, at: (0, at[0] * 4 + i)),
    ]
    args = [hidden, weight]
    if got is not None:
        specs.append(pl.BlockSpec((1, count, SHARE), piece))
        args.append(got)
    return pl.pallas_call(
        down_first_kernel if got is None else down_second_kernel,
        grid_spec=pltpu.PrefetchScalarGridSpec(
            num_scalar_prefetch=1,
            grid=(4,),
            in_specs=specs,
            out_specs=pl.BlockSpec((1, count, SHARE), piece),
        ),
        out_shape=jax.ShapeDtypeStruct((4, count, SHARE), BF16),
        compiler_params=pltpu.CompilerParams(vmem_limit_bytes=VMEM_LIMIT),
        cost_estimate=pl.CostEstimate(flops=2 * count * units * HALF, bytes_accessed=9_000_000, transcendentals=0),
    )(at, *args)


def mix_kernel(at_ref, tok_ref, mix_ref, rows_ref, out_ref):
    total = tok_ref[...].astype(F32)
    for source in range(rows_ref.shape[0]):
        total += jnp.dot(mix_ref[...], rows_ref[source], preferred_element_type=F32)
    out_ref[...] = total.astype(BF16)


def mix(at, tokens, mix_matrix, rows):
    whole = lambda i, at: (0, 0)
    return pl.pallas_call(
        mix_kernel,
        grid_spec=pltpu.PrefetchScalarGridSpec(
            num_scalar_prefetch=1,
            grid=(1,),
            in_specs=[
                pl.BlockSpec((TOK_DEV, SHARE), lambda i, at: (0, at[0])),
                pl.BlockSpec((TOK_DEV, ROWS), whole),
                pl.BlockSpec(rows.shape, lambda i, at: (0, 0, 0)),
            ],
            out_specs=pl.BlockSpec((TOK_DEV, SHARE), whole),
        ),
        out_shape=jax.ShapeDtypeStruct((TOK_DEV, SHARE), BF16),
        compiler_params=pltpu.CompilerParams(vmem_limit_bytes=VMEM_LIMIT),
        cost_estimate=pl.CostEstimate(flops=8 * TOK_DEV * ROWS * SHARE, bytes_accessed=4_000_000, transcendentals=0),
    )(at, tokens, mix_matrix, rows)


def swap(values):
    return lax.ppermute(values, "pp", [(0, 1), (1, 0)])


def spread_copies(values, axis):
    count = lax.axis_size(axis)
    copies = jnp.broadcast_to(values[None], (count,) + values.shape)
    return lax.all_to_all(copies, axis, split_axis=0, concat_axis=0, tiled=True)


def on_device(tokens, norm_gain, router_weight, expert_ids, up_weight, down_weight):
    core = lax.axis_index("pp").astype(jnp.int32)
    own, other = core.reshape(1), (1 - core).reshape(1)
    share = (core * 4 + lax.axis_index("dp").astype(jnp.int32)).reshape(1)
    up = up_weight.reshape(2, HALF, up_weight.shape[2])
    down = down_weight[0]

    outgoing, mix_matrix = route(tokens, norm_gain, router_weight, expert_ids)
    mine = lax.all_to_all(outgoing.reshape(EXPERTS, CAP, HALF), "ep", split_axis=0, concat_axis=0, tiled=True).reshape(ROWS, HALF)
    theirs = swap(mine)
    part = up_half(own, mine, up)
    hidden = up_half(other, theirs, up, part)
    got = swap(down_half(other, hidden, down))
    total = down_half(own, hidden, down, got)
    returned = lax.all_to_all(
        total.reshape(4 * EXPERTS, CAP, SHARE), ("dp", "ep"), split_axis=0, concat_axis=0, tiled=True
    ).reshape(4, ROWS, SHARE)
    piece = mix(share, tokens, mix_matrix, returned)
    pieces = spread_copies(spread_copies(piece, "dp"), "pp")
    return jnp.transpose(pieces, (2, 0, 1, 3)).reshape(TOK_DEV, D)


def solution(mesh):
    in_specs = (
        P("ep", None),
        P(),
        P(),
        P("ep", None),
        P("ep", None, ("pp", "dp")),
        P("ep", ("pp", "dp"), None),
    )
    return jax.shard_map(on_device, mesh=mesh, in_specs=in_specs, out_specs=P("ep", None), check_vma=False)
```

```python
import jax
import jax.numpy as jnp
from jax import lax
from jax.experimental import pallas as pl
from jax.experimental.pallas import tpu as pltpu
from jax.sharding import PartitionSpec as P

D = 3072
EXPERTS = 16
TOP = 4
TOK_DEV = 256
CAP = 72
ROWS = EXPERTS * CAP
HALF = D // 2
WIDE = 512
THIN = 256
Z_STEPS = (0, 2, 1, 3)
EPSILON = 1e-05
F32 = jnp.float32
BF16 = jnp.bfloat16
ROUTE_VMEM = 60 * 1024 * 1024
MATMUL_VMEM = 16 * 1024 * 1024
NT = (((1,), (1,)), ((), ()))


def route_kernel(tok_ref, gain_ref, router_ref, ids_ref, buf_ref, mix_ref, normed_ref, key_ref):
    step = pl.program_id(0)
    experts_a_step = EXPERTS // pl.num_programs(0)

    @pl.when(step == 0)
    def _():
        def norm_rows(part, carry):
            rows = pl.ds(pl.multiple_of(part * 32, 32), 32)
            values = tok_ref[rows, :].astype(F32)
            shifted = values - jnp.mean(values, axis=-1, keepdims=True)
            spread = jnp.mean(shifted * shifted, axis=-1, keepdims=True)
            normed = (shifted * lax.rsqrt(spread + EPSILON) * gain_ref[...]).astype(BF16)
            normed_ref[0, rows, :] = normed[:, :HALF]
            normed_ref[1, rows, :] = normed[:, HALF:]
            return carry

        lax.fori_loop(0, TOK_DEV // 32, norm_rows, 0)
        logits = lax.dot_general(normed_ref[0], router_ref[:, :HALF], NT, preferred_element_type=F32)
        logits += lax.dot_general(normed_ref[1], router_ref[:, HALF:], NT, preferred_element_type=F32)

        named = jnp.zeros((EXPERTS, TOK_DEV), jnp.int32)
        expert = lax.broadcasted_iota(jnp.int32, (EXPERTS, TOK_DEV), 0)
        for k in range(TOP):
            named += (ids_ref[k : k + 1, :] == expert).astype(jnp.int32)
        named = named.astype(F32)
        row = lax.broadcasted_iota(jnp.int32, (TOK_DEV, TOK_DEV), 0)
        col = lax.broadcasted_iota(jnp.int32, (TOK_DEV, TOK_DEV), 1)
        earlier = (row > col).astype(F32).astype(BF16)
        same = (row == col).astype(F32).astype(BF16)
        named_bf = named.astype(BF16)
        place_t = lax.dot_general(named_bf, earlier, NT, preferred_element_type=F32)
        key_ref[...] = jnp.where(named > 0.5, place_t, -1.0)
        place = lax.dot_general(earlier, named_bf, NT, preferred_element_type=F32)
        chosen = lax.dot_general(same, named_bf, NT, preferred_element_type=F32) > 0.5
        key = jnp.where(chosen, place, -1.0)
        weight = jnp.where(chosen, jnp.exp(logits), 0.0)
        gate = weight / jnp.sum(weight, axis=1, keepdims=True)

        slot = lax.broadcasted_iota(jnp.int32, (EXPERTS, ROWS), 1)
        first = lax.broadcasted_iota(jnp.int32, (EXPERTS, ROWS), 0) * CAP
        inside = (slot >= first) & (slot < first + CAP)
        spread_out = inside.astype(F32).astype(BF16)
        slot_in = jnp.sum(jnp.where(inside, slot - first, 0).astype(F32), axis=0, keepdims=True)
        key_wide = jnp.dot(key.astype(BF16), spread_out, preferred_element_type=F32)
        gate_wide = jnp.dot(gate.astype(BF16), spread_out, preferred_element_type=F32)
        mix_ref[...] = jnp.where(key_wide == slot_in, gate_wide, 0.0).astype(BF16)

    keys = key_ref[pl.ds(pl.multiple_of(step * experts_a_step, experts_a_step), experts_a_step), :]
    slot_row = lax.broadcasted_iota(jnp.int32, (CAP, TOK_DEV), 0).astype(F32)
    picks = [(slot_row == keys[e : e + 1, :]).astype(F32) for e in range(experts_a_step)]
    pick = jnp.concatenate(picks, axis=0).astype(BF16)
    buf_ref[...] = jnp.dot(pick, normed_ref[lax.axis_index("pp")], preferred_element_type=F32).astype(BF16)


def route(tokens, norm_gain, router_weight, expert_ids):
    steps = 2
    whole = lambda i: (0, 0)
    return pl.pallas_call(
        route_kernel,
        grid=(steps,),
        in_specs=[
            pl.BlockSpec((TOK_DEV, D), whole),
            pl.BlockSpec((1, D), whole),
            pl.BlockSpec((EXPERTS, D), whole),
            pl.BlockSpec((TOP, TOK_DEV), whole),
        ],
        out_specs=[
            pl.BlockSpec((ROWS // steps, HALF), lambda i: (i, 0)),
            pl.BlockSpec((TOK_DEV, ROWS), whole),
        ],
        out_shape=[
            jax.ShapeDtypeStruct((ROWS, HALF), BF16),
            jax.ShapeDtypeStruct((TOK_DEV, ROWS), BF16),
        ],
        scratch_shapes=[
            pltpu.VMEM((2, TOK_DEV, HALF), BF16),
            pltpu.VMEM((EXPERTS, TOK_DEV), F32),
        ],
        compiler_params=pltpu.CompilerParams(vmem_limit_bytes=ROUTE_VMEM),
        cost_estimate=pl.CostEstimate(flops=2 * ROWS * TOK_DEV * HALF, bytes_accessed=6_000_000, transcendentals=0),
    )(tokens, norm_gain.reshape(1, D), router_weight.T, expert_ids.T)


def up_first_kernel(at_ref, x_ref, w_ref, out_ref):
    out_ref[...] = jnp.dot(x_ref[...], w_ref[0], preferred_element_type=F32)


def up_second_kernel(at_ref, x_ref, w_ref, part_ref, out_ref):
    value = part_ref[...] + jnp.dot(x_ref[...], w_ref[0], preferred_element_type=F32)
    out_ref[...] = (value / (1.0 + jnp.exp(-value))).astype(BF16)


def up_half(at, rows_in, weight, part=None):
    count, inner = rows_in.shape
    units = weight.shape[2]
    block = count // 4
    row_block = lambda i, at: (i, 0)
    specs = [pl.BlockSpec((block, inner), row_block), pl.BlockSpec((1, inner, units), lambda i, at: (at[0], 0, 0))]
    args = [rows_in, weight]
    if part is not None:
        specs.append(pl.BlockSpec((block, units), row_block))
        args.append(part)
    return pl.pallas_call(
        up_first_kernel if part is None else up_second_kernel,
        grid_spec=pltpu.PrefetchScalarGridSpec(
            num_scalar_prefetch=1,
            grid=(4,),
            in_specs=specs,
            out_specs=pl.BlockSpec((block, units), row_block),
        ),
        out_shape=jax.ShapeDtypeStruct((count, units), F32 if part is None else BF16),
        compiler_params=pltpu.CompilerParams(vmem_limit_bytes=MATMUL_VMEM),
        cost_estimate=pl.CostEstimate(flops=2 * count * inner * units, bytes_accessed=9_000_000, transcendentals=0),
    )(at, *args)


def down_first_kernel(at_ref, h_ref, w_ref, out_ref):
    out_ref[0] = jnp.dot(h_ref[...], w_ref[...], preferred_element_type=F32).astype(BF16)


def down_second_kernel(at_ref, h_ref, w_ref, got_ref, *out_refs):
    value = jnp.dot(h_ref[...], w_ref[...], preferred_element_type=F32)
    value = (value + got_ref[0].astype(F32)).astype(BF16)
    for piece, out_ref in enumerate(out_refs):

        @pl.when(pl.program_id(0) == piece)
        def _(out_ref=out_ref):
            out_ref[...] = value


def down_part(blocks, hidden, weight, width, got=None):
    count, units = hidden.shape
    parts = blocks.shape[0]
    piece = pl.BlockSpec((1, count, width), lambda i, at: (i, 0, 0))
    specs = [
        pl.BlockSpec((count, units), lambda i, at: (0, 0)),
        pl.BlockSpec((units, width), lambda i, at: (0, at[i])),
    ]
    args = [hidden, weight]
    if got is None:
        out_specs, out_shape = piece, jax.ShapeDtypeStruct((parts, count, width), BF16)
    else:
        specs.append(piece)
        args.append(got)
        out_specs = [pl.BlockSpec((count, width), lambda i, at: (0, 0))] * parts
        out_shape = [jax.ShapeDtypeStruct((count, width), BF16)] * parts
    return pl.pallas_call(
        down_first_kernel if got is None else down_second_kernel,
        grid_spec=pltpu.PrefetchScalarGridSpec(num_scalar_prefetch=1, grid=(parts,), in_specs=specs, out_specs=out_specs),
        out_shape=out_shape,
        compiler_params=pltpu.CompilerParams(vmem_limit_bytes=MATMUL_VMEM),
        cost_estimate=pl.CostEstimate(flops=2 * count * units * width * parts, bytes_accessed=6_000_000, transcendentals=0),
    )(blocks, *args)


def mix_kernel(mix_ref, rows_ref, out_ref):
    out_ref[...] = jnp.dot(mix_ref[...], rows_ref[...], preferred_element_type=F32).astype(BF16)


def mix_add_kernel(at_ref, tok_ref, mix_ref, rows_ref, out_ref):
    total = jnp.dot(mix_ref[...], rows_ref[...], preferred_element_type=F32)
    out_ref[...] = (tok_ref[...].astype(F32) + total).astype(BF16)


def mix(mix_matrix, rows):
    return pl.pallas_call(
        mix_kernel,
        out_shape=jax.ShapeDtypeStruct((TOK_DEV, rows.shape[1]), BF16),
        compiler_params=pltpu.CompilerParams(vmem_limit_bytes=MATMUL_VMEM),
        cost_estimate=pl.CostEstimate(flops=2 * TOK_DEV * rows.size, bytes_accessed=2_000_000, transcendentals=0),
    )(mix_matrix, rows)


def mix_add(at, tokens, mix_matrix, rows):
    whole = lambda i, at: (0, 0)
    width = rows.shape[1]
    return pl.pallas_call(
        mix_add_kernel,
        grid_spec=pltpu.PrefetchScalarGridSpec(
            num_scalar_prefetch=1,
            grid=(1,),
            in_specs=[
                pl.BlockSpec((TOK_DEV, width), lambda i, at: (0, at[0])),
                pl.BlockSpec((TOK_DEV, ROWS), whole),
                pl.BlockSpec(rows.shape, whole),
            ],
            out_specs=pl.BlockSpec((TOK_DEV, width), whole),
        ),
        out_shape=jax.ShapeDtypeStruct((TOK_DEV, width), BF16),
        compiler_params=pltpu.CompilerParams(vmem_limit_bytes=MATMUL_VMEM),
        cost_estimate=pl.CostEstimate(flops=2 * TOK_DEV * rows.size, bytes_accessed=2_000_000, transcendentals=0),
    )(at, tokens, mix_matrix, rows)


def assemble_kernel(at_ref, *refs):
    pieces, out_ref, sems = refs[:-2], refs[-2], refs[-1]
    copies = []
    for i, piece in enumerate(pieces):
        start = pl.multiple_of(at_ref[i] * 256, 256)
        copies.append(pltpu.make_async_copy(piece, out_ref.at[:, pl.ds(start, piece.shape[1])], sems.at[i]))
    for copy in copies:
        copy.start()
    for copy in copies:
        copy.wait()


def assemble(at, pieces):
    return pl.pallas_call(
        assemble_kernel,
        in_specs=[pl.BlockSpec(memory_space=pltpu.SMEM)] + [pl.BlockSpec(memory_space=pl.ANY)] * len(pieces),
        out_specs=pl.BlockSpec(memory_space=pl.ANY),
        out_shape=jax.ShapeDtypeStruct((TOK_DEV, D), BF16),
        scratch_shapes=[pltpu.SemaphoreType.DMA((len(pieces),))],
        compiler_params=pltpu.CompilerParams(vmem_limit_bytes=MATMUL_VMEM),
        cost_estimate=pl.CostEstimate(flops=0, bytes_accessed=3_000_000, transcendentals=0),
    )(at, *pieces)


def swap(values):
    return lax.ppermute(values, "pp", [(0, 1), (1, 0)])


def along_z(values, step):
    count = lax.axis_size("dp")
    return lax.ppermute(values, "dp", [(i, (i + step) % count) for i in range(count)])


def to_experts(rows):
    width = rows.shape[1]
    return lax.all_to_all(rows.reshape(EXPERTS, CAP, width), "ep", split_axis=0, concat_axis=0, tiled=True).reshape(ROWS, width)


def on_device(tokens, norm_gain, router_weight, expert_ids, up_weight, down_weight):
    core = lax.axis_index("pp").astype(jnp.int32)
    z = lax.axis_index("dp").astype(jnp.int32)
    other = 1 - core
    steps = jnp.array(Z_STEPS, jnp.int32)
    ranks = (z + steps) % 4
    up = up_weight.reshape(2, HALF, up_weight.shape[2])
    down = down_weight[0]

    outgoing, mix_matrix = route(tokens, norm_gain, router_weight, expert_ids)
    mine = to_experts(outgoing)
    theirs = swap(mine)
    part = up_half(core.reshape(1), mine, up)
    hidden = up_half(other.reshape(1), theirs, up, part)

    got_wide = swap(down_part((other * 3).reshape(1), hidden, down, WIDE))
    got_thin = swap(down_part(other * 6 + 2 + ranks, hidden, down, THIN))
    (wide,) = down_part((core * 3).reshape(1), hidden, down, WIDE, got_wide)
    thin = down_part(core * 6 + 2 + ranks, hidden, down, THIN, got_thin)
    thin_sum = thin[0].astype(F32)
    for piece, step in zip(thin[1:], Z_STEPS[1:]):
        thin_sum = thin_sum + along_z(piece, step).astype(F32)
    wide_part = mix(mix_matrix, to_experts(wide))
    thin_own = mix_add((core * 6 + 2 + z).reshape(1), tokens, mix_matrix, to_experts(thin_sum.astype(BF16)))

    wide_own = lax.dynamic_slice(tokens, (0, core * HALF), (TOK_DEV, WIDE)).astype(F32) + wide_part.astype(F32)
    for step in Z_STEPS[1:]:
        wide_own = wide_own + along_z(wide_part, step).astype(F32)
    wide_own = wide_own.astype(BF16)
    thin_all = [thin_own] + [along_z(thin_own, step) for step in Z_STEPS[1:]]
    pieces = [wide_own, swap(wide_own)] + thin_all + [swap(piece) for piece in thin_all]
    sources = (z - steps) % 4
    places = jnp.concatenate([jnp.stack([core * 6, other * 6]), core * 6 + 2 + sources, other * 6 + 2 + sources])
    return assemble(places.astype(jnp.int32), pieces)


def solution(mesh):
    in_specs = (
        P("ep", None),
        P(),
        P(),
        P("ep", None),
        P("ep", None, ("pp", "dp")),
        P("ep", ("pp", "dp"), None),
    )
    return jax.shard_map(on_device, mesh=mesh, in_specs=in_specs, out_specs=P("ep", None), check_vma=False)
```

```python
import jax
import jax.numpy as jnp
from jax import lax
from jax.experimental import pallas as pl
from jax.experimental.pallas import tpu as pltpu
from jax.sharding import PartitionSpec as P

D = 3072
EXPERTS = 16
TOP = 4
TOK_DEV = 256
CAP = 72
ROWS = EXPERTS * CAP
HALF = D // 2
WIDE = 512
THIN = 256
Z_STEPS = (2, 1, 3, 0)
EPSILON = 1e-05
F32 = jnp.float32
BF16 = jnp.bfloat16
ROUTE_VMEM = 60 * 1024 * 1024
MATMUL_VMEM = 16 * 1024 * 1024
NT = (((1,), (1,)), ((), ()))


def route_kernel(tok_ref, gain_ref, router_ref, ids_ref, buf_ref, mix_ref, normed_ref, key_ref):
    step = pl.program_id(0)
    experts_a_step = EXPERTS // pl.num_programs(0)

    @pl.when(step == 0)
    def _():
        def norm_rows(part, carry):
            rows = pl.ds(pl.multiple_of(part * 32, 32), 32)
            values = tok_ref[rows, :].astype(F32)
            shifted = values - jnp.mean(values, axis=-1, keepdims=True)
            spread = jnp.mean(shifted * shifted, axis=-1, keepdims=True)
            normed = (shifted * lax.rsqrt(spread + EPSILON) * gain_ref[...]).astype(BF16)
            normed_ref[0, rows, :] = normed[:, :HALF]
            normed_ref[1, rows, :] = normed[:, HALF:]
            return carry

        lax.fori_loop(0, TOK_DEV // 32, norm_rows, 0)
        logits = lax.dot_general(normed_ref[0], router_ref[:, :HALF], NT, preferred_element_type=F32)
        logits += lax.dot_general(normed_ref[1], router_ref[:, HALF:], NT, preferred_element_type=F32)

        named = jnp.zeros((EXPERTS, TOK_DEV), jnp.int32)
        expert = lax.broadcasted_iota(jnp.int32, (EXPERTS, TOK_DEV), 0)
        for k in range(TOP):
            named += (ids_ref[k : k + 1, :] == expert).astype(jnp.int32)
        named = named.astype(F32)
        row = lax.broadcasted_iota(jnp.int32, (TOK_DEV, TOK_DEV), 0)
        col = lax.broadcasted_iota(jnp.int32, (TOK_DEV, TOK_DEV), 1)
        earlier = (row > col).astype(F32).astype(BF16)
        same = (row == col).astype(F32).astype(BF16)
        named_bf = named.astype(BF16)
        place_t = lax.dot_general(named_bf, earlier, NT, preferred_element_type=F32)
        key_ref[...] = jnp.where(named > 0.5, place_t, -1.0)
        place = lax.dot_general(earlier, named_bf, NT, preferred_element_type=F32)
        chosen = lax.dot_general(same, named_bf, NT, preferred_element_type=F32) > 0.5
        key = jnp.where(chosen, place, -1.0)
        weight = jnp.where(chosen, jnp.exp(logits), 0.0)
        gate = weight / jnp.sum(weight, axis=1, keepdims=True)

        slot = lax.broadcasted_iota(jnp.int32, (EXPERTS, ROWS), 1)
        first = lax.broadcasted_iota(jnp.int32, (EXPERTS, ROWS), 0) * CAP
        inside = (slot >= first) & (slot < first + CAP)
        spread_out = inside.astype(F32).astype(BF16)
        slot_in = jnp.sum(jnp.where(inside, slot - first, 0).astype(F32), axis=0, keepdims=True)
        key_wide = jnp.dot(key.astype(BF16), spread_out, preferred_element_type=F32)
        gate_wide = jnp.dot(gate.astype(BF16), spread_out, preferred_element_type=F32)
        mix_ref[...] = jnp.where(key_wide == slot_in, gate_wide, 0.0).astype(BF16)

    keys = key_ref[pl.ds(pl.multiple_of(step * experts_a_step, experts_a_step), experts_a_step), :]
    slot_row = lax.broadcasted_iota(jnp.int32, (CAP, TOK_DEV), 0).astype(F32)
    picks = [(slot_row == keys[e : e + 1, :]).astype(F32) for e in range(experts_a_step)]
    pick = jnp.concatenate(picks, axis=0).astype(BF16)
    buf_ref[...] = jnp.dot(pick, normed_ref[lax.axis_index("pp")], preferred_element_type=F32).astype(BF16)


def route(tokens, norm_gain, router_weight, expert_ids):
    steps = 2
    whole = lambda i: (0, 0)
    return pl.pallas_call(
        route_kernel,
        grid=(steps,),
        in_specs=[
            pl.BlockSpec((TOK_DEV, D), whole),
            pl.BlockSpec((1, D), whole),
            pl.BlockSpec((EXPERTS, D), whole),
            pl.BlockSpec((TOP, TOK_DEV), whole),
        ],
        out_specs=[
            pl.BlockSpec((ROWS // steps, HALF), lambda i: (i, 0)),
            pl.BlockSpec((TOK_DEV, ROWS), whole),
        ],
        out_shape=[
            jax.ShapeDtypeStruct((ROWS, HALF), BF16),
            jax.ShapeDtypeStruct((TOK_DEV, ROWS), BF16),
        ],
        scratch_shapes=[
            pltpu.VMEM((2, TOK_DEV, HALF), BF16),
            pltpu.VMEM((EXPERTS, TOK_DEV), F32),
        ],
        compiler_params=pltpu.CompilerParams(vmem_limit_bytes=ROUTE_VMEM),
        cost_estimate=pl.CostEstimate(flops=2 * ROWS * TOK_DEV * HALF, bytes_accessed=6_000_000, transcendentals=0),
    )(tokens, norm_gain.reshape(1, D), router_weight.T, expert_ids.T)


def product(rows, weight):
    return jnp.dot(rows, weight, preferred_element_type=F32)


def columns(weight, start, width):
    return lax.dynamic_slice_in_dim(weight, start, width, axis=1)


def mix_kernel(mix_ref, rows_ref, out_ref):
    out_ref[...] = jnp.dot(mix_ref[...], rows_ref[...], preferred_element_type=F32).astype(BF16)


def mix_add_kernel(tok_ref, mix_ref, rows_ref, out_ref):
    total = jnp.dot(mix_ref[...], rows_ref[...], preferred_element_type=F32)
    out_ref[...] = (tok_ref[...].astype(F32) + total).astype(BF16)


def mix(mix_matrix, rows):
    return pl.pallas_call(
        mix_kernel,
        out_shape=jax.ShapeDtypeStruct((TOK_DEV, rows.shape[1]), BF16),
        compiler_params=pltpu.CompilerParams(vmem_limit_bytes=MATMUL_VMEM),
        cost_estimate=pl.CostEstimate(flops=2 * TOK_DEV * rows.size, bytes_accessed=2_000_000, transcendentals=0),
    )(mix_matrix, rows)


def mix_add(tokens, mix_matrix, rows):
    return pl.pallas_call(
        mix_add_kernel,
        out_shape=jax.ShapeDtypeStruct((TOK_DEV, rows.shape[1]), BF16),
        compiler_params=pltpu.CompilerParams(vmem_limit_bytes=MATMUL_VMEM),
        cost_estimate=pl.CostEstimate(flops=2 * TOK_DEV * rows.size, bytes_accessed=2_000_000, transcendentals=0),
    )(tokens, mix_matrix, rows)


def assemble_kernel(at_ref, *refs):
    pieces, out_ref, sems = refs[:-2], refs[-2], refs[-1]
    copies = []
    for i, piece in enumerate(pieces):
        start = pl.multiple_of(at_ref[i] * 256, 256)
        copies.append(pltpu.make_async_copy(piece, out_ref.at[:, pl.ds(start, piece.shape[1])], sems.at[i]))
    for copy in copies:
        copy.start()
    for copy in copies:
        copy.wait()


def assemble(at, pieces):
    return pl.pallas_call(
        assemble_kernel,
        in_specs=[pl.BlockSpec(memory_space=pltpu.SMEM)] + [pl.BlockSpec(memory_space=pl.ANY)] * len(pieces),
        out_specs=pl.BlockSpec(memory_space=pl.ANY),
        out_shape=jax.ShapeDtypeStruct((TOK_DEV, D), BF16),
        scratch_shapes=[pltpu.SemaphoreType.DMA((len(pieces),))],
        compiler_params=pltpu.CompilerParams(vmem_limit_bytes=MATMUL_VMEM),
        cost_estimate=pl.CostEstimate(flops=0, bytes_accessed=3_000_000, transcendentals=0),
    )(at, *pieces)


def swap(values):
    return lax.ppermute(values, "pp", [(0, 1), (1, 0)])


def along_z(values, step):
    count = lax.axis_size("dp")
    return lax.ppermute(values, "dp", [(i, (i + step) % count) for i in range(count)])


def to_experts(rows):
    width = rows.shape[1]
    return lax.all_to_all(rows.reshape(EXPERTS, CAP, width), "ep", split_axis=0, concat_axis=0, tiled=True).reshape(ROWS, width)


def on_device(tokens, norm_gain, router_weight, expert_ids, up_weight, down_weight):
    core = lax.axis_index("pp").astype(jnp.int32)
    z = lax.axis_index("dp").astype(jnp.int32)
    other = 1 - core
    up = up_weight.reshape(2, HALF, up_weight.shape[2])
    down = down_weight[0]

    outgoing, mix_matrix = route(tokens, norm_gain, router_weight, expert_ids)
    token_wide = lax.dynamic_slice(tokens, (0, core * HALF), (TOK_DEV, WIDE))
    token_thin = lax.dynamic_slice(tokens, (0, core * HALF + WIDE + z * THIN), (TOK_DEV, THIN))
    token_wide, token_thin = lax.optimization_barrier((token_wide, token_thin))
    mine = to_experts(outgoing)
    theirs = swap(mine)
    hidden = jax.nn.silu(product(mine, up[core]) + product(theirs, up[other])).astype(BF16)

    def partial_sums(start, width):
        got = swap(product(hidden, columns(down, other * HALF + start, width)).astype(BF16))
        return (product(hidden, columns(down, core * HALF + start, width)) + got.astype(F32)).astype(BF16)

    thin = [partial_sums(WIDE + rank * THIN, THIN) for rank in [(z + step) % 4 for step in Z_STEPS]]
    wide = partial_sums(0, WIDE)
    thin_sum = thin[-1].astype(F32)
    for piece, step in zip(thin[:-1], Z_STEPS[:-1]):
        thin_sum = thin_sum + along_z(piece, step).astype(F32)
    wide_rows, thin_sum = lax.optimization_barrier((to_experts(wide), thin_sum.astype(BF16)))
    wide_part = mix(mix_matrix, wide_rows)
    thin_own = mix_add(token_thin, mix_matrix, to_experts(thin_sum))

    wide_own = token_wide.astype(F32) + wide_part.astype(F32)
    for step in Z_STEPS[:-1]:
        wide_own = wide_own + along_z(wide_part, step).astype(F32)
    wide_own = wide_own.astype(BF16)
    thin_all = [along_z(thin_own, step) for step in Z_STEPS[:-1]] + [thin_own]
    pieces = [wide_own, swap(wide_own)] + thin_all + [swap(piece) for piece in thin_all]
    sources = (z - jnp.array(Z_STEPS, jnp.int32)) % 4
    places = jnp.concatenate([jnp.stack([core * 6, other * 6]), core * 6 + 2 + sources, other * 6 + 2 + sources])
    return assemble(places.astype(jnp.int32), pieces)


def solution(mesh):
    in_specs = (
        P("ep", None),
        P(),
        P(),
        P("ep", None),
        P("ep", None, ("pp", "dp")),
        P("ep", ("pp", "dp"), None),
    )
    return jax.shard_map(on_device, mesh=mesh, in_specs=in_specs, out_specs=P("ep", None), check_vma=False)
```

```python
import jax
import jax.numpy as jnp
from jax import lax
from jax.experimental import pallas as pl
from jax.experimental.pallas import tpu as pltpu
from jax.sharding import PartitionSpec as P

D = 3072
EXPERTS = 16
TOP = 4
TOK_DEV = 256
CAP = 72
ROWS = EXPERTS * CAP
HALF = D // 2
WIDE = 512
THIN = 256
Z_STEPS = (1, 3, 2, 0)
EPSILON = 1e-05
F32 = jnp.float32
BF16 = jnp.bfloat16
ROUTE_VMEM = 60 * 1024 * 1024
MATMUL_VMEM = 16 * 1024 * 1024
ROUTE_BLOCK = 128
NORM_STEPS = TOK_DEV // ROUTE_BLOCK
PICK_STEPS = 2
PICK = EXPERTS // PICK_STEPS
NORM_ROWS = 16
NT = (((1,), (1,)), ((), ()))


def slot_rows(keys):
    slot = lax.broadcasted_iota(jnp.int32, (CAP, TOK_DEV), 0).astype(F32)
    return jnp.concatenate([(slot == keys[e : e + 1, :]).astype(F32) for e in range(keys.shape[0])], axis=0).astype(BF16)


def route_kernel(tok_ref, gain_ref, router_ref, ids_ref, rows_ref, mix_ref, normed_ref, key_t_ref):
    step = pl.program_id(0)
    core = lax.axis_index("pp")

    def norm_rows(part, carry):
        inner = pl.ds(pl.multiple_of(part * NORM_ROWS, NORM_ROWS), NORM_ROWS)
        outer = pl.ds(pl.multiple_of(step * ROUTE_BLOCK + part * NORM_ROWS, NORM_ROWS), NORM_ROWS)
        values = tok_ref[inner, :].astype(F32)
        shifted = values - jnp.mean(values, axis=-1, keepdims=True)
        spread = jnp.mean(shifted * shifted, axis=-1, keepdims=True)
        normed = (shifted * lax.rsqrt(spread + EPSILON) * gain_ref[...]).astype(BF16)
        normed_ref[0, outer, :] = normed[:, :HALF]
        normed_ref[1, outer, :] = normed[:, HALF:]
        return carry

    @pl.when(step < NORM_STEPS)
    def _():
        lax.fori_loop(0, ROUTE_BLOCK // NORM_ROWS, norm_rows, 0, unroll=True)

    @pl.when(step == NORM_STEPS - 1)
    def _():
        named = jnp.zeros((EXPERTS, TOK_DEV), jnp.int32)
        expert = lax.broadcasted_iota(jnp.int32, (EXPERTS, TOK_DEV), 0)
        for k in range(TOP):
            named += (ids_ref[k : k + 1, :] == expert).astype(jnp.int32)
        named = named.astype(F32)
        row = lax.broadcasted_iota(jnp.int32, (TOK_DEV, TOK_DEV), 0)
        col = lax.broadcasted_iota(jnp.int32, (TOK_DEV, TOK_DEV), 1)
        earlier = (row > col).astype(F32).astype(BF16)
        same = (row == col).astype(F32).astype(BF16)
        named_bf = named.astype(BF16)
        place_t = lax.dot_general(named_bf, earlier, NT, preferred_element_type=F32)
        key_t = jnp.where(named > 0.5, place_t, -1.0)
        key_t_ref[...] = key_t
        logits = lax.dot_general(normed_ref[0], router_ref[:, :HALF], NT, preferred_element_type=F32)
        logits += lax.dot_general(normed_ref[1], router_ref[:, HALF:], NT, preferred_element_type=F32)
        place = lax.dot_general(earlier, named_bf, NT, preferred_element_type=F32)
        chosen = lax.dot_general(same, named_bf, NT, preferred_element_type=F32) > 0.5
        weight = jnp.where(chosen, jnp.exp(logits), 0.0)
        key = jnp.where(chosen, place, -1.0)
        gate = weight / jnp.sum(weight, axis=1, keepdims=True)

        slot = lax.broadcasted_iota(jnp.int32, (EXPERTS, ROWS), 1)
        first = lax.broadcasted_iota(jnp.int32, (EXPERTS, ROWS), 0) * CAP
        inside = (slot >= first) & (slot < first + CAP)
        spread_out = inside.astype(F32).astype(BF16)
        slot_in = jnp.sum(jnp.where(inside, slot - first, 0).astype(F32), axis=0, keepdims=True)
        key_wide = jnp.dot(key.astype(BF16), spread_out, preferred_element_type=F32)
        gate_wide = jnp.dot(gate.astype(BF16), spread_out, preferred_element_type=F32)
        mix_ref[...] = jnp.where(key_wide == slot_in, gate_wide, 0.0).astype(BF16)

    @pl.when(step >= NORM_STEPS - 1)
    def _():
        keys = key_t_ref[pl.ds(pl.multiple_of((step - NORM_STEPS + 1) * PICK, PICK), PICK), :]
        rows_ref[...] = jnp.dot(slot_rows(keys), normed_ref[core], preferred_element_type=F32).astype(BF16)


def route(tokens, norm_gain, router_weight, expert_ids):
    whole = lambda i: (0, 0)
    shapes = [((ROWS, HALF), BF16), ((TOK_DEV, ROWS), BF16)]
    return pl.pallas_call(
        route_kernel,
        grid=(NORM_STEPS + PICK_STEPS - 1,),
        in_specs=[
            pl.BlockSpec((ROUTE_BLOCK, D), lambda i: (jnp.minimum(i, NORM_STEPS - 1), 0)),
            pl.BlockSpec((1, D), whole),
            pl.BlockSpec((EXPERTS, D), whole),
            pl.BlockSpec((TOP, TOK_DEV), whole),
        ],
        out_specs=[
            pl.BlockSpec((PICK * CAP, HALF), lambda i: (jnp.maximum(i - NORM_STEPS + 1, 0), 0)),
            pl.BlockSpec((TOK_DEV, ROWS), whole),
        ],
        out_shape=[jax.ShapeDtypeStruct(shape, kind) for shape, kind in shapes],
        scratch_shapes=[pltpu.VMEM((2, TOK_DEV, HALF), BF16), pltpu.VMEM((EXPERTS, TOK_DEV), F32)],
        compiler_params=pltpu.CompilerParams(vmem_limit_bytes=ROUTE_VMEM),
        cost_estimate=pl.CostEstimate(flops=2 * ROWS * TOK_DEV * HALF, bytes_accessed=6_000_000, transcendentals=0),
    )(tokens, norm_gain.reshape(1, D), router_weight.T, expert_ids.T)


def product(rows, weight):
    return jnp.dot(rows, weight, preferred_element_type=F32)


def columns(weight, start, width):
    return lax.dynamic_slice_in_dim(weight, start, width, axis=1)


def mix_kernel(mix_ref, rows_ref, out_ref):
    out_ref[...] = jnp.dot(mix_ref[...], rows_ref[...], preferred_element_type=F32).astype(BF16)


def mix_add_kernel(tok_ref, mix_ref, rows_ref, out_ref):
    total = jnp.dot(mix_ref[...], rows_ref[...], preferred_element_type=F32)
    out_ref[...] = (tok_ref[...].astype(F32) + total).astype(BF16)


def mix(mix_matrix, rows):
    return pl.pallas_call(
        mix_kernel,
        out_shape=jax.ShapeDtypeStruct((TOK_DEV, rows.shape[1]), BF16),
        compiler_params=pltpu.CompilerParams(vmem_limit_bytes=MATMUL_VMEM),
        cost_estimate=pl.CostEstimate(flops=2 * TOK_DEV * rows.size, bytes_accessed=2_000_000, transcendentals=0),
    )(mix_matrix, rows)


def mix_add(tokens, mix_matrix, rows):
    return pl.pallas_call(
        mix_add_kernel,
        out_shape=jax.ShapeDtypeStruct((TOK_DEV, rows.shape[1]), BF16),
        compiler_params=pltpu.CompilerParams(vmem_limit_bytes=MATMUL_VMEM),
        cost_estimate=pl.CostEstimate(flops=2 * TOK_DEV * rows.size, bytes_accessed=2_000_000, transcendentals=0),
    )(tokens, mix_matrix, rows)


def assemble_kernel(at_ref, *refs):
    pieces, out_ref, sems = refs[:-2], refs[-2], refs[-1]
    copies = []
    for i, piece in enumerate(pieces):
        start = pl.multiple_of(at_ref[i] * 256, 256)
        copies.append(pltpu.make_async_copy(piece, out_ref.at[:, pl.ds(start, piece.shape[1])], sems.at[i]))
    for copy in copies:
        copy.start()
    for copy in copies:
        copy.wait()


def assemble(at, pieces):
    return pl.pallas_call(
        assemble_kernel,
        in_specs=[pl.BlockSpec(memory_space=pltpu.SMEM)] + [pl.BlockSpec(memory_space=pl.ANY)] * len(pieces),
        out_specs=pl.BlockSpec(memory_space=pl.ANY),
        out_shape=jax.ShapeDtypeStruct((TOK_DEV, D), BF16),
        scratch_shapes=[pltpu.SemaphoreType.DMA((len(pieces),))],
        compiler_params=pltpu.CompilerParams(vmem_limit_bytes=MATMUL_VMEM),
        cost_estimate=pl.CostEstimate(flops=0, bytes_accessed=3_000_000, transcendentals=0),
    )(at, *pieces)


def swap(values):
    return lax.ppermute(values, "pp", [(0, 1), (1, 0)])


def along_z(values, step):
    count = lax.axis_size("dp")
    return lax.ppermute(values, "dp", [(i, (i + step) % count) for i in range(count)])


def to_experts(rows):
    width = rows.shape[1]
    return lax.all_to_all(rows.reshape(EXPERTS, CAP, width), "ep", split_axis=0, concat_axis=0, tiled=True).reshape(ROWS, width)


def after(earlier, values):
    return lax.optimization_barrier((earlier, values))[1]


def on_device(tokens, norm_gain, router_weight, expert_ids, up_weight, down_weight):
    core = lax.axis_index("pp").astype(jnp.int32)
    z = lax.axis_index("dp").astype(jnp.int32)
    other = 1 - core
    up = up_weight.reshape(2, HALF, up_weight.shape[2])
    down = down_weight[0]

    outgoing, mix_matrix = route(tokens, norm_gain, router_weight, expert_ids)
    token_wide = lax.dynamic_slice(tokens, (0, core * HALF), (TOK_DEV, WIDE))
    token_thin = lax.dynamic_slice(tokens, (0, core * HALF + WIDE + z * THIN), (TOK_DEV, THIN))
    token_wide, token_thin = lax.optimization_barrier((token_wide, token_thin))
    mine = to_experts(outgoing)
    theirs = swap(mine)
    hidden = jax.nn.silu(product(mine, up[core]) + product(theirs, up[other])).astype(BF16)

    def partial_sums(start, width):
        got = swap(product(hidden, columns(down, other * HALF + start, width)).astype(BF16))
        return (product(hidden, columns(down, core * HALF + start, width)) + got.astype(F32)).astype(BF16)

    thin = [partial_sums(WIDE + rank * THIN, THIN) for rank in [(z + step) % 4 for step in Z_STEPS]]
    wide = partial_sums(0, WIDE)
    thin_sum = thin[-1].astype(F32)
    for piece, step in zip(thin[:-1], Z_STEPS[:-1]):
        thin_sum = thin_sum + along_z(piece, step).astype(F32)
    wide_rows, thin_sum = lax.optimization_barrier((to_experts(wide), thin_sum.astype(BF16)))
    wide_part = mix(mix_matrix, wide_rows)
    thin_own = mix_add(token_thin, mix_matrix, to_experts(thin_sum))

    wide_own = token_wide.astype(F32) + wide_part.astype(F32)
    for step in Z_STEPS[:-1]:
        wide_own = wide_own + along_z(wide_part, step).astype(F32)
    wide_own = wide_own.astype(BF16)
    thin_all = [along_z(thin_own, step) for step in Z_STEPS[:-1]] + [thin_own]
    pieces = [wide_own, swap(wide_own)] + thin_all + [swap(piece) for piece in thin_all]
    sources = (z - jnp.array(Z_STEPS, jnp.int32)) % 4
    places = jnp.concatenate([jnp.stack([core * 6, other * 6]), core * 6 + 2 + sources, other * 6 + 2 + sources])
    return assemble(places.astype(jnp.int32), pieces)


def solution(mesh):
    in_specs = (
        P("ep", None),
        P(),
        P(),
        P("ep", None),
        P("ep", None, ("pp", "dp")),
        P("ep", ("pp", "dp"), None),
    )
    return jax.shard_map(on_device, mesh=mesh, in_specs=in_specs, out_specs=P("ep", None), check_vma=False)
```

```python
import jax
import jax.numpy as jnp
from jax import lax
from jax.experimental import pallas as pl
from jax.experimental.pallas import tpu as pltpu
from jax.sharding import PartitionSpec as P

D = 3072
EXPERTS = 16
TOP = 4
TOK_DEV = 256
CAP = 72
ROWS = EXPERTS * CAP
HALF = D // 2
WIDE = 512
THIN = 256
Z_STEPS = (1, 3, 2, 0)
EPSILON = 1e-05
F32 = jnp.float32
BF16 = jnp.bfloat16
ROUTE_VMEM = 60 * 1024 * 1024
MATMUL_VMEM = 6 * 1024 * 1024
ROUTE_BLOCK = 64
PICK = 4
NORM_ROWS = 16
NT = (((1,), (1,)), ((), ()))


def slot_rows(keys):
    slot = lax.broadcasted_iota(jnp.int32, (CAP, TOK_DEV), 0).astype(F32)
    return jnp.concatenate([(slot == keys[e : e + 1, :]).astype(F32) for e in range(keys.shape[0])], axis=0).astype(BF16)


def route_kernel(tok_hbm, gain_hbm, router_hbm, ids_hbm, rows_hbm, mix_hbm, tok_ref, gain_ref, router_ref, ids_ref, normed_ref, rows_ref, mix_ref, sems, out_sems):
    small = [
        pltpu.make_async_copy(ids_hbm, ids_ref, sems.at[0]),
        pltpu.make_async_copy(gain_hbm, gain_ref, sems.at[1]),
        pltpu.make_async_copy(router_hbm, router_ref, sems.at[2]),
    ]
    blocks = [pl.ds(begin, ROUTE_BLOCK) for begin in range(0, TOK_DEV, ROUTE_BLOCK)]
    loads = [pltpu.make_async_copy(tok_hbm.at[block], tok_ref.at[block], sems.at[3 + i]) for i, block in enumerate(blocks)]
    for copy in small[:2] + loads + small[2:]:
        copy.start()

    small[0].wait()
    named = jnp.zeros((EXPERTS, TOK_DEV), jnp.int32)
    expert = lax.broadcasted_iota(jnp.int32, (EXPERTS, TOK_DEV), 0)
    for k in range(TOP):
        named += (ids_ref[k : k + 1, :] == expert).astype(jnp.int32)
    named = named.astype(F32)
    row = lax.broadcasted_iota(jnp.int32, (TOK_DEV, TOK_DEV), 0)
    col = lax.broadcasted_iota(jnp.int32, (TOK_DEV, TOK_DEV), 1)
    earlier = (row > col).astype(F32).astype(BF16)
    same = (row == col).astype(F32).astype(BF16)
    named_bf = named.astype(BF16)
    place_t = lax.dot_general(named_bf, earlier, NT, preferred_element_type=F32)
    key_t = jnp.where(named > 0.5, place_t, -1.0)
    place = lax.dot_general(earlier, named_bf, NT, preferred_element_type=F32)
    chosen = lax.dot_general(same, named_bf, NT, preferred_element_type=F32) > 0.5
    key = jnp.where(chosen, place, -1.0)

    def norm_rows(part, carry):
        rows = pl.ds(pl.multiple_of(part * NORM_ROWS, NORM_ROWS), NORM_ROWS)
        values = tok_ref[rows, :].astype(F32)
        shifted = values - jnp.mean(values, axis=-1, keepdims=True)
        spread = jnp.mean(shifted * shifted, axis=-1, keepdims=True)
        normed = (shifted * lax.rsqrt(spread + EPSILON) * gain_ref[...]).astype(BF16)
        normed_ref[0, rows, :] = normed[:, :HALF]
        normed_ref[1, rows, :] = normed[:, HALF:]
        return carry

    small[1].wait()
    turns = ROUTE_BLOCK // NORM_ROWS
    for i, copy in enumerate(loads):
        copy.wait()
        lax.fori_loop(i * turns, (i + 1) * turns, norm_rows, 0, unroll=True)

    core = lax.axis_index("pp")
    stores = []
    for i in range(EXPERTS // PICK):
        rows = pl.ds(i * PICK * CAP, PICK * CAP)
        pick = slot_rows(key_t[i * PICK : (i + 1) * PICK, :])
        rows_ref[rows, :] = jnp.dot(pick, normed_ref[core], preferred_element_type=F32).astype(BF16)
        stores.append(pltpu.make_async_copy(rows_ref.at[rows], rows_hbm.at[rows], out_sems.at[i]))
        stores[-1].start()

    small[2].wait()
    logits = lax.dot_general(normed_ref[0], router_ref[:, :HALF], NT, preferred_element_type=F32)
    logits += lax.dot_general(normed_ref[1], router_ref[:, HALF:], NT, preferred_element_type=F32)
    weight = jnp.where(chosen, jnp.exp(logits), 0.0)
    gate = weight / jnp.sum(weight, axis=1, keepdims=True)
    slot = lax.broadcasted_iota(jnp.int32, (EXPERTS, ROWS), 1)
    first = lax.broadcasted_iota(jnp.int32, (EXPERTS, ROWS), 0) * CAP
    inside = (slot >= first) & (slot < first + CAP)
    spread_out = inside.astype(F32).astype(BF16)
    slot_in = jnp.sum(jnp.where(inside, slot - first, 0).astype(F32), axis=0, keepdims=True)
    key_wide = jnp.dot(key.astype(BF16), spread_out, preferred_element_type=F32)
    gate_wide = jnp.dot(gate.astype(BF16), spread_out, preferred_element_type=F32)
    mix_ref[...] = jnp.where(key_wide == slot_in, gate_wide, 0.0).astype(BF16)
    stores.append(pltpu.make_async_copy(mix_ref, mix_hbm, out_sems.at[EXPERTS // PICK]))
    stores[-1].start()
    for copy in stores:
        copy.wait()


def route(tokens, norm_gain, router_weight, expert_ids):
    shapes = [((ROWS, HALF), BF16), ((TOK_DEV, ROWS), BF16)]
    held = [((TOK_DEV, D), BF16), ((1, D), F32), ((EXPERTS, D), BF16), ((TOP, TOK_DEV), jnp.int32), ((2, TOK_DEV, HALF), BF16)]
    anywhere = pl.BlockSpec(memory_space=pl.ANY)
    return pl.pallas_call(
        route_kernel,
        in_specs=[anywhere] * 4,
        out_specs=[anywhere] * 2,
        out_shape=[jax.ShapeDtypeStruct(shape, kind) for shape, kind in shapes],
        scratch_shapes=[pltpu.VMEM(shape, kind) for shape, kind in held + shapes]
        + [pltpu.SemaphoreType.DMA((3 + TOK_DEV // ROUTE_BLOCK,)), pltpu.SemaphoreType.DMA((EXPERTS // PICK + 1,))],
        compiler_params=pltpu.CompilerParams(vmem_limit_bytes=ROUTE_VMEM),
        cost_estimate=pl.CostEstimate(flops=2 * ROWS * TOK_DEV * HALF, bytes_accessed=6_000_000, transcendentals=0),
    )(tokens, norm_gain.reshape(1, D), router_weight.T, expert_ids.T)


def product(rows, weight):
    return jnp.dot(rows, weight, preferred_element_type=F32)


def columns(weight, start, width):
    return lax.dynamic_slice_in_dim(weight, start, width, axis=1)


def mix_kernel(mix_ref, rows_ref, out_ref):
    out_ref[...] = jnp.dot(mix_ref[...], rows_ref[...], preferred_element_type=F32).astype(BF16)


def mix_add_kernel(tok_ref, mix_ref, rows_ref, out_ref):
    total = jnp.dot(mix_ref[...], rows_ref[...], preferred_element_type=F32)
    out_ref[...] = (tok_ref[...].astype(F32) + total).astype(BF16)


def mix(mix_matrix, rows):
    return pl.pallas_call(
        mix_kernel,
        out_shape=jax.ShapeDtypeStruct((TOK_DEV, rows.shape[1]), BF16),
        compiler_params=pltpu.CompilerParams(vmem_limit_bytes=MATMUL_VMEM),
        cost_estimate=pl.CostEstimate(flops=2 * TOK_DEV * rows.size, bytes_accessed=2_000_000, transcendentals=0),
    )(mix_matrix, rows)


def mix_add(tokens, mix_matrix, rows):
    return pl.pallas_call(
        mix_add_kernel,
        out_shape=jax.ShapeDtypeStruct((TOK_DEV, rows.shape[1]), BF16),
        compiler_params=pltpu.CompilerParams(vmem_limit_bytes=MATMUL_VMEM),
        cost_estimate=pl.CostEstimate(flops=2 * TOK_DEV * rows.size, bytes_accessed=2_000_000, transcendentals=0),
    )(tokens, mix_matrix, rows)


def assemble_kernel(at_ref, *refs):
    pieces, out_ref, sems = refs[:-2], refs[-2], refs[-1]
    copies = []
    for i, piece in enumerate(pieces):
        start = pl.multiple_of(at_ref[i] * 256, 256)
        copies.append(pltpu.make_async_copy(piece, out_ref.at[:, pl.ds(start, piece.shape[1])], sems.at[i]))
    for copy in copies:
        copy.start()
    for copy in copies:
        copy.wait()


def assemble(at, pieces):
    return pl.pallas_call(
        assemble_kernel,
        in_specs=[pl.BlockSpec(memory_space=pltpu.SMEM)] + [pl.BlockSpec(memory_space=pl.ANY)] * len(pieces),
        out_specs=pl.BlockSpec(memory_space=pl.ANY),
        out_shape=jax.ShapeDtypeStruct((TOK_DEV, D), BF16),
        scratch_shapes=[pltpu.SemaphoreType.DMA((len(pieces),))],
        compiler_params=pltpu.CompilerParams(vmem_limit_bytes=MATMUL_VMEM),
        cost_estimate=pl.CostEstimate(flops=0, bytes_accessed=3_000_000, transcendentals=0),
    )(at, *pieces)


def swap(values):
    return lax.ppermute(values, "pp", [(0, 1), (1, 0)])


def along_z(values, step):
    count = lax.axis_size("dp")
    return lax.ppermute(values, "dp", [(i, (i + step) % count) for i in range(count)])


def to_experts(rows):
    width = rows.shape[1]
    return lax.all_to_all(rows.reshape(EXPERTS, CAP, width), "ep", split_axis=0, concat_axis=0, tiled=True).reshape(ROWS, width)


def silu(value):
    return 0.5 * value * (1.0 + jnp.tanh(0.5 * value))


def after(earlier, values):
    return lax.optimization_barrier((earlier, values))[1]


def on_device(tokens, norm_gain, router_weight, expert_ids, up_weight, down_weight):
    core = lax.axis_index("pp").astype(jnp.int32)
    z = lax.axis_index("dp").astype(jnp.int32)
    other = 1 - core
    up = up_weight.reshape(2, HALF, up_weight.shape[2])
    down = down_weight[0]

    outgoing, mix_matrix = route(tokens, norm_gain, router_weight, expert_ids)
    token_wide = lax.dynamic_slice(tokens, (0, core * HALF), (TOK_DEV, WIDE))
    token_thin = lax.dynamic_slice(tokens, (0, core * HALF + WIDE + z * THIN), (TOK_DEV, THIN))
    mine = to_experts(outgoing)
    theirs = swap(mine)
    hidden = silu(product(mine, up[core]) + product(theirs, up[other])).astype(BF16)

    def partial_sums(start, width):
        got = swap(product(hidden, columns(down, other * HALF + start, width)).astype(BF16))
        return (product(hidden, columns(down, core * HALF + start, width)) + got.astype(F32)).astype(BF16)

    def place(step):
        return WIDE + (z + step) % 4 * THIN

    sent = [partial_sums(place(step), THIN) for step in Z_STEPS[:-1]]
    arrived = [along_z(piece, step) for piece, step in zip(sent, Z_STEPS[:-1])]
    wide = partial_sums(0, WIDE)
    kept = partial_sums(place(0), THIN)
    thin_sum = lax.optimization_barrier(kept).astype(F32)
    for piece in arrived:
        thin_sum = thin_sum + piece.astype(F32)
    wide_rows, thin_sum = lax.optimization_barrier((to_experts(wide), thin_sum.astype(BF16)))
    wide_part = mix(mix_matrix, wide_rows)
    thin_own = mix_add(token_thin, mix_matrix, to_experts(thin_sum))

    wide_own = token_wide.astype(F32) + wide_part.astype(F32)
    for step in Z_STEPS[:-1]:
        wide_own = wide_own + along_z(wide_part, step).astype(F32)
    wide_own = wide_own.astype(BF16)
    thin_all = [along_z(thin_own, step) for step in Z_STEPS[:-1]] + [thin_own]
    pieces = [wide_own, swap(wide_own)] + thin_all + [swap(piece) for piece in thin_all]
    sources = (z - jnp.array(Z_STEPS, jnp.int32)) % 4
    places = jnp.concatenate([jnp.stack([core * 6, other * 6]), core * 6 + 2 + sources, other * 6 + 2 + sources])
    return assemble(places.astype(jnp.int32), pieces)


def solution(mesh):
    in_specs = (
        P("ep", None),
        P(),
        P(),
        P("ep", None),
        P("ep", None, ("pp", "dp")),
        P("ep", ("pp", "dp"), None),
    )
    return jax.shard_map(on_device, mesh=mesh, in_specs=in_specs, out_specs=P("ep", None), check_vma=False)
```

```python
import jax
import jax.numpy as jnp
from jax import lax
from jax.experimental import pallas as pl
from jax.experimental.pallas import tpu as pltpu
from jax.sharding import PartitionSpec as P

D = 3072
EXPERTS = 16
TOP = 4
TOK_DEV = 256
CAP = 72
ROWS = EXPERTS * CAP
HALF = D // 2
WIDE = 512
THIN = 256
Z_STEPS = (1, 3, 2, 0)
TAIL_STEPS = (2, 1, 3, 0)
EPSILON = 1e-05
F32 = jnp.float32
BF16 = jnp.bfloat16
ROUTE_VMEM = 60 * 1024 * 1024
MATMUL_VMEM = 6 * 1024 * 1024
ROUTE_BLOCK = 64
PICK = 4
NORM_ROWS = 16
NT = (((1,), (1,)), ((), ()))


def slot_rows(keys):
    slot = lax.broadcasted_iota(jnp.int32, (CAP, TOK_DEV), 0).astype(F32)
    return jnp.concatenate([(slot == keys[e : e + 1, :]).astype(F32) for e in range(keys.shape[0])], axis=0).astype(BF16)


def route_kernel(tok_hbm, gain_hbm, router_hbm, ids_hbm, rows_hbm, mix_hbm, tok_ref, gain_ref, router_ref, ids_ref, normed_ref, rows_ref, mix_ref, sems, out_sems):
    small = [
        pltpu.make_async_copy(ids_hbm, ids_ref, sems.at[0]),
        pltpu.make_async_copy(gain_hbm, gain_ref, sems.at[1]),
        pltpu.make_async_copy(router_hbm, router_ref, sems.at[2]),
    ]
    blocks = [pl.ds(begin, ROUTE_BLOCK) for begin in range(0, TOK_DEV, ROUTE_BLOCK)]
    loads = [pltpu.make_async_copy(tok_hbm.at[block], tok_ref.at[block], sems.at[3 + i]) for i, block in enumerate(blocks)]
    for copy in small[:2] + loads + small[2:]:
        copy.start()

    small[0].wait()
    named = jnp.zeros((EXPERTS, TOK_DEV), jnp.int32)
    expert = lax.broadcasted_iota(jnp.int32, (EXPERTS, TOK_DEV), 0)
    for k in range(TOP):
        named += (ids_ref[k : k + 1, :] == expert).astype(jnp.int32)
    named = named.astype(F32)
    row = lax.broadcasted_iota(jnp.int32, (TOK_DEV, TOK_DEV), 0)
    col = lax.broadcasted_iota(jnp.int32, (TOK_DEV, TOK_DEV), 1)
    earlier = (row > col).astype(F32).astype(BF16)
    same = (row == col).astype(F32).astype(BF16)
    named_bf = named.astype(BF16)
    place_t = lax.dot_general(named_bf, earlier, NT, preferred_element_type=F32)
    key_t = jnp.where(named > 0.5, place_t, -1.0)
    place = lax.dot_general(earlier, named_bf, NT, preferred_element_type=F32)
    chosen = lax.dot_general(same, named_bf, NT, preferred_element_type=F32) > 0.5
    key = jnp.where(chosen, place, -1.0)

    def norm_rows(part, carry):
        rows = pl.ds(pl.multiple_of(part * NORM_ROWS, NORM_ROWS), NORM_ROWS)
        values = tok_ref[rows, :].astype(F32)
        shifted = values - jnp.mean(values, axis=-1, keepdims=True)
        spread = jnp.mean(shifted * shifted, axis=-1, keepdims=True)
        normed = (shifted * lax.rsqrt(spread + EPSILON) * gain_ref[...]).astype(BF16)
        normed_ref[0, rows, :] = normed[:, :HALF]
        normed_ref[1, rows, :] = normed[:, HALF:]
        return carry

    small[1].wait()
    turns = ROUTE_BLOCK // NORM_ROWS
    for i, copy in enumerate(loads):
        copy.wait()
        lax.fori_loop(i * turns, (i + 1) * turns, norm_rows, 0, unroll=True)

    core = lax.axis_index("pp")
    stores = []
    for i in range(EXPERTS // PICK):
        rows = pl.ds(i * PICK * CAP, PICK * CAP)
        pick = slot_rows(key_t[i * PICK : (i + 1) * PICK, :])
        rows_ref[rows, :] = jnp.dot(pick, normed_ref[core], preferred_element_type=F32).astype(BF16)
        stores.append(pltpu.make_async_copy(rows_ref.at[rows], rows_hbm.at[rows], out_sems.at[i]))
        stores[-1].start()

    small[2].wait()
    logits = lax.dot_general(normed_ref[0], router_ref[:, :HALF], NT, preferred_element_type=F32)
    logits += lax.dot_general(normed_ref[1], router_ref[:, HALF:], NT, preferred_element_type=F32)
    weight = jnp.where(chosen, jnp.exp(logits), 0.0)
    gate = weight / jnp.sum(weight, axis=1, keepdims=True)
    slot = lax.broadcasted_iota(jnp.int32, (EXPERTS, ROWS), 1)
    first = lax.broadcasted_iota(jnp.int32, (EXPERTS, ROWS), 0) * CAP
    inside = (slot >= first) & (slot < first + CAP)
    spread_out = inside.astype(F32).astype(BF16)
    slot_in = jnp.sum(jnp.where(inside, slot - first, 0).astype(F32), axis=0, keepdims=True)
    key_wide = jnp.dot(key.astype(BF16), spread_out, preferred_element_type=F32)
    gate_wide = jnp.dot(gate.astype(BF16), spread_out, preferred_element_type=F32)
    mix_ref[...] = jnp.where(key_wide == slot_in, gate_wide, 0.0).astype(BF16)
    stores.append(pltpu.make_async_copy(mix_ref, mix_hbm, out_sems.at[EXPERTS // PICK]))
    stores[-1].start()
    for copy in stores:
        copy.wait()


def route(tokens, norm_gain, router_weight, expert_ids):
    shapes = [((ROWS, HALF), BF16), ((TOK_DEV, ROWS), BF16)]
    held = [((TOK_DEV, D), BF16), ((1, D), F32), ((EXPERTS, D), BF16), ((TOP, TOK_DEV), jnp.int32), ((2, TOK_DEV, HALF), BF16)]
    anywhere = pl.BlockSpec(memory_space=pl.ANY)
    return pl.pallas_call(
        route_kernel,
        in_specs=[anywhere] * 4,
        out_specs=[anywhere] * 2,
        out_shape=[jax.ShapeDtypeStruct(shape, kind) for shape, kind in shapes],
        scratch_shapes=[pltpu.VMEM(shape, kind) for shape, kind in held + shapes]
        + [pltpu.SemaphoreType.DMA((3 + TOK_DEV // ROUTE_BLOCK,)), pltpu.SemaphoreType.DMA((EXPERTS // PICK + 1,))],
        compiler_params=pltpu.CompilerParams(vmem_limit_bytes=ROUTE_VMEM),
        cost_estimate=pl.CostEstimate(flops=2 * ROWS * TOK_DEV * HALF, bytes_accessed=6_000_000, transcendentals=0),
    )(tokens, norm_gain.reshape(1, D), router_weight.T, expert_ids.T)


def product(rows, weight):
    return jnp.dot(rows, weight, preferred_element_type=F32)


def columns(weight, start, width):
    return lax.dynamic_slice_in_dim(weight, start, width, axis=1)


def mix_kernel(mix_ref, rows_ref, out_ref):
    out_ref[...] = jnp.dot(mix_ref[...], rows_ref[...], preferred_element_type=F32).astype(BF16)


def mix_add_kernel(tok_ref, mix_ref, rows_ref, out_ref):
    total = jnp.dot(mix_ref[...], rows_ref[...], preferred_element_type=F32)
    out_ref[...] = (tok_ref[...].astype(F32) + total).astype(BF16)


def mix(mix_matrix, rows):
    return pl.pallas_call(
        mix_kernel,
        out_shape=jax.ShapeDtypeStruct((TOK_DEV, rows.shape[1]), BF16),
        compiler_params=pltpu.CompilerParams(vmem_limit_bytes=MATMUL_VMEM),
        cost_estimate=pl.CostEstimate(flops=2 * TOK_DEV * rows.size, bytes_accessed=2_000_000, transcendentals=0),
    )(mix_matrix, rows)


def mix_add(tokens, mix_matrix, rows):
    return pl.pallas_call(
        mix_add_kernel,
        out_shape=jax.ShapeDtypeStruct((TOK_DEV, rows.shape[1]), BF16),
        compiler_params=pltpu.CompilerParams(vmem_limit_bytes=MATMUL_VMEM),
        cost_estimate=pl.CostEstimate(flops=2 * TOK_DEV * rows.size, bytes_accessed=2_000_000, transcendentals=0),
    )(tokens, mix_matrix, rows)


def assemble_kernel(at_ref, *refs):
    pieces, out_ref, sems = refs[:-2], refs[-2], refs[-1]
    copies = []
    for i, piece in enumerate(pieces):
        start = pl.multiple_of(at_ref[i] * 256, 256)
        copies.append(pltpu.make_async_copy(piece, out_ref.at[:, pl.ds(start, piece.shape[1])], sems.at[i]))
    for copy in copies:
        copy.start()
    for copy in copies:
        copy.wait()


def assemble(at, pieces):
    return pl.pallas_call(
        assemble_kernel,
        in_specs=[pl.BlockSpec(memory_space=pltpu.SMEM)] + [pl.BlockSpec(memory_space=pl.ANY)] * len(pieces),
        out_specs=pl.BlockSpec(memory_space=pl.ANY),
        out_shape=jax.ShapeDtypeStruct((TOK_DEV, D), BF16),
        scratch_shapes=[pltpu.SemaphoreType.DMA((len(pieces),))],
        compiler_params=pltpu.CompilerParams(vmem_limit_bytes=MATMUL_VMEM),
        cost_estimate=pl.CostEstimate(flops=0, bytes_accessed=3_000_000, transcendentals=0),
    )(at, *pieces)


def swap(values):
    return lax.ppermute(values, "pp", [(0, 1), (1, 0)])


def along_z(values, step):
    count = lax.axis_size("dp")
    return lax.ppermute(values, "dp", [(i, (i + step) % count) for i in range(count)])


def to_experts(rows):
    width = rows.shape[1]
    return lax.all_to_all(rows.reshape(EXPERTS, CAP, width), "ep", split_axis=0, concat_axis=0, tiled=True).reshape(ROWS, width)


def silu(value):
    return 0.5 * value * (1.0 + jnp.tanh(0.5 * value))


def after(earlier, values):
    return lax.optimization_barrier((earlier, values))[1]


def on_device(tokens, norm_gain, router_weight, expert_ids, up_weight, down_weight):
    core = lax.axis_index("pp").astype(jnp.int32)
    z = lax.axis_index("dp").astype(jnp.int32)
    other = 1 - core
    up = up_weight.reshape(2, HALF, up_weight.shape[2])
    down = down_weight[0]

    outgoing, mix_matrix = route(tokens, norm_gain, router_weight, expert_ids)
    token_wide = lax.dynamic_slice(tokens, (0, core * HALF), (TOK_DEV, WIDE))
    token_thin = lax.dynamic_slice(tokens, (0, core * HALF + WIDE + z * THIN), (TOK_DEV, THIN))
    mine = to_experts(outgoing)
    theirs = swap(mine)
    hidden = silu(product(mine, up[core]) + product(theirs, up[other])).astype(BF16)

    def partial_sums(start, width):
        got = swap(product(hidden, columns(down, other * HALF + start, width)).astype(BF16))
        return (product(hidden, columns(down, core * HALF + start, width)) + got.astype(F32)).astype(BF16)

    def place(step):
        return WIDE + (z + step) % 4 * THIN

    sent = [partial_sums(place(step), THIN) for step in Z_STEPS[:-1]]
    arrived = [along_z(piece, step) for piece, step in zip(sent, Z_STEPS[:-1])]
    wide = partial_sums(0, WIDE)
    kept = partial_sums(place(0), THIN)
    thin_sum = lax.optimization_barrier(kept).astype(F32)
    for piece in arrived:
        thin_sum = thin_sum + piece.astype(F32)
    wide_rows, thin_sum = lax.optimization_barrier((to_experts(wide), thin_sum.astype(BF16)))
    wide_part = mix(mix_matrix, wide_rows)
    thin_own = mix_add(token_thin, mix_matrix, to_experts(thin_sum))

    wide_own = token_wide.astype(F32) + wide_part.astype(F32)
    for step in Z_STEPS[:-1]:
        wide_own = wide_own + along_z(wide_part, step).astype(F32)
    wide_own = wide_own.astype(BF16)
    thin_all = [along_z(thin_own, step) for step in TAIL_STEPS[:-1]] + [thin_own]
    pieces = [wide_own, swap(wide_own)] + thin_all + [swap(piece) for piece in thin_all]
    sources = (z - jnp.array(TAIL_STEPS, jnp.int32)) % 4
    places = jnp.concatenate([jnp.stack([core * 6, other * 6]), core * 6 + 2 + sources, other * 6 + 2 + sources])
    return assemble(places.astype(jnp.int32), pieces)


def solution(mesh):
    in_specs = (
        P("ep", None),
        P(),
        P(),
        P("ep", None),
        P("ep", None, ("pp", "dp")),
        P("ep", ("pp", "dp"), None),
    )
    return jax.shard_map(on_device, mesh=mesh, in_specs=in_specs, out_specs=P("ep", None), check_vma=False)
```

```python
import jax
import jax.numpy as jnp
from jax import lax
from jax.experimental import pallas as pl
from jax.experimental.pallas import tpu as pltpu
from jax.sharding import PartitionSpec as P

D = 3072
EXPERTS = 16
TOP = 4
TOK_DEV = 256
CAP = 72
ROWS = EXPERTS * CAP
HALF = D // 2
WIDE = 512
THIN = 256
Z_STEPS = (1, 3, 2, 0)
TAIL_STEPS = (2, 1, 3, 0)
EPSILON = 1e-05
F32 = jnp.float32
BF16 = jnp.bfloat16
ROUTE_VMEM = 60 * 1024 * 1024
MATMUL_VMEM = 6 * 1024 * 1024
ROUTE_BLOCK = 128
PICK = 2
NORM_ROWS = 16
NT = (((1,), (1,)), ((), ()))


def slot_rows(keys):
    slot = lax.broadcasted_iota(jnp.int32, (CAP, TOK_DEV), 0).astype(F32)
    return jnp.concatenate([(slot == keys[e : e + 1, :]).astype(F32) for e in range(keys.shape[0])], axis=0).astype(BF16)


def route_kernel(tok_hbm, gain_hbm, router_hbm, ids_hbm, rows_hbm, key_hbm, gate_hbm, tok_ref, gain_ref, router_ref, ids_ref, normed_ref, rows_ref, key_ref, gate_ref, sems, out_sems):
    small = [
        pltpu.make_async_copy(ids_hbm, ids_ref, sems.at[0]),
        pltpu.make_async_copy(gain_hbm, gain_ref, sems.at[1]),
        pltpu.make_async_copy(router_hbm, router_ref, sems.at[2]),
    ]
    blocks = [pl.ds(begin, ROUTE_BLOCK) for begin in range(0, TOK_DEV, ROUTE_BLOCK)]
    loads = [pltpu.make_async_copy(tok_hbm.at[block], tok_ref.at[block], sems.at[3 + i]) for i, block in enumerate(blocks)]
    for copy in small[:2] + loads + small[2:]:
        copy.start()

    small[0].wait()
    named = jnp.zeros((EXPERTS, TOK_DEV), jnp.int32)
    expert = lax.broadcasted_iota(jnp.int32, (EXPERTS, TOK_DEV), 0)
    for k in range(TOP):
        named += (ids_ref[k : k + 1, :] == expert).astype(jnp.int32)
    named = named.astype(F32)
    row = lax.broadcasted_iota(jnp.int32, (TOK_DEV, TOK_DEV), 0)
    col = lax.broadcasted_iota(jnp.int32, (TOK_DEV, TOK_DEV), 1)
    earlier = (row > col).astype(F32).astype(BF16)
    same = (row == col).astype(F32).astype(BF16)
    named_bf = named.astype(BF16)
    place_t = lax.dot_general(named_bf, earlier, NT, preferred_element_type=F32)
    key_t = jnp.where(named > 0.5, place_t, -1.0)
    place = lax.dot_general(earlier, named_bf, NT, preferred_element_type=F32)
    chosen = lax.dot_general(same, named_bf, NT, preferred_element_type=F32) > 0.5
    key = jnp.where(chosen, place, -1.0)

    def norm_rows(part, carry):
        rows = pl.ds(pl.multiple_of(part * NORM_ROWS, NORM_ROWS), NORM_ROWS)
        values = tok_ref[rows, :].astype(F32)
        shifted = values - jnp.mean(values, axis=-1, keepdims=True)
        spread = jnp.mean(shifted * shifted, axis=-1, keepdims=True)
        normed = (shifted * lax.rsqrt(spread + EPSILON) * gain_ref[...]).astype(BF16)
        normed_ref[0, rows, :] = normed[:, :HALF]
        normed_ref[1, rows, :] = normed[:, HALF:]
        return carry

    small[1].wait()
    turns = ROUTE_BLOCK // NORM_ROWS
    for i, copy in enumerate(loads):
        copy.wait()
        lax.fori_loop(i * turns, (i + 1) * turns, norm_rows, 0, unroll=True)

    core = lax.axis_index("pp")
    stores = []
    for i in range(EXPERTS // PICK):
        rows = pl.ds(i * PICK * CAP, PICK * CAP)
        pick = slot_rows(key_t[i * PICK : (i + 1) * PICK, :])
        rows_ref[rows, :] = jnp.dot(pick, normed_ref[core], preferred_element_type=F32).astype(BF16)
        stores.append(pltpu.make_async_copy(rows_ref.at[rows], rows_hbm.at[rows], out_sems.at[i]))
        stores[-1].start()

    small[2].wait()
    logits = lax.dot_general(normed_ref[0], router_ref[:, :HALF], NT, preferred_element_type=F32)
    logits += lax.dot_general(normed_ref[1], router_ref[:, HALF:], NT, preferred_element_type=F32)
    weight = jnp.where(chosen, jnp.exp(logits), 0.0)
    gate = weight / jnp.sum(weight, axis=1, keepdims=True)
    key_ref[...] = key
    gate_ref[...] = gate
    for i, (here, there) in enumerate(((key_ref, key_hbm), (gate_ref, gate_hbm))):
        stores.append(pltpu.make_async_copy(here, there, out_sems.at[EXPERTS // PICK + i]))
        stores[-1].start()
    for copy in stores:
        copy.wait()


def route(tokens, norm_gain, router_weight, expert_ids):
    shapes = [((ROWS, HALF), BF16), ((TOK_DEV, EXPERTS), F32), ((TOK_DEV, EXPERTS), F32)]
    held = [((TOK_DEV, D), BF16), ((1, D), F32), ((EXPERTS, D), BF16), ((TOP, TOK_DEV), jnp.int32), ((2, TOK_DEV, HALF), BF16)]
    anywhere = pl.BlockSpec(memory_space=pl.ANY)
    return pl.pallas_call(
        route_kernel,
        in_specs=[anywhere] * 4,
        out_specs=[anywhere] * 3,
        out_shape=[jax.ShapeDtypeStruct(shape, kind) for shape, kind in shapes],
        scratch_shapes=[pltpu.VMEM(shape, kind) for shape, kind in held + shapes]
        + [pltpu.SemaphoreType.DMA((3 + TOK_DEV // ROUTE_BLOCK,)), pltpu.SemaphoreType.DMA((EXPERTS // PICK + 2,))],
        compiler_params=pltpu.CompilerParams(vmem_limit_bytes=ROUTE_VMEM),
        cost_estimate=pl.CostEstimate(flops=2 * ROWS * TOK_DEV * HALF, bytes_accessed=6_000_000, transcendentals=0),
    )(tokens, norm_gain.reshape(1, D), router_weight.T, expert_ids.T)


def mix_matrix_kernel(key_ref, gate_ref, mix_ref):
    slot = lax.broadcasted_iota(jnp.int32, (EXPERTS, ROWS), 1)
    first = lax.broadcasted_iota(jnp.int32, (EXPERTS, ROWS), 0) * CAP
    inside = (slot >= first) & (slot < first + CAP)
    spread_out = inside.astype(F32).astype(BF16)
    slot_in = jnp.sum(jnp.where(inside, slot - first, 0).astype(F32), axis=0, keepdims=True)
    key_wide = jnp.dot(key_ref[...].astype(BF16), spread_out, preferred_element_type=F32)
    gate_wide = jnp.dot(gate_ref[...].astype(BF16), spread_out, preferred_element_type=F32)
    mix_ref[...] = jnp.where(key_wide == slot_in, gate_wide, 0.0).astype(BF16)


def mix_matrix_of(key, gate):
    return pl.pallas_call(
        mix_matrix_kernel,
        out_shape=jax.ShapeDtypeStruct((TOK_DEV, ROWS), BF16),
        compiler_params=pltpu.CompilerParams(vmem_limit_bytes=MATMUL_VMEM),
        cost_estimate=pl.CostEstimate(flops=4 * ROWS * TOK_DEV * EXPERTS, bytes_accessed=1_000_000, transcendentals=0),
    )(key, gate)


def product(rows, weight):
    return jnp.dot(rows, weight, preferred_element_type=F32)


def columns(weight, start, width):
    return lax.dynamic_slice_in_dim(weight, start, width, axis=1)


def mix_kernel(mix_ref, rows_ref, out_ref):
    out_ref[...] = jnp.dot(mix_ref[...], rows_ref[...], preferred_element_type=F32).astype(BF16)


def mix_add_kernel(tok_ref, mix_ref, rows_ref, out_ref):
    total = jnp.dot(mix_ref[...], rows_ref[...], preferred_element_type=F32)
    out_ref[...] = (tok_ref[...].astype(F32) + total).astype(BF16)


def mix(mix_matrix, rows):
    return pl.pallas_call(
        mix_kernel,
        out_shape=jax.ShapeDtypeStruct((TOK_DEV, rows.shape[1]), BF16),
        compiler_params=pltpu.CompilerParams(vmem_limit_bytes=MATMUL_VMEM),
        cost_estimate=pl.CostEstimate(flops=2 * TOK_DEV * rows.size, bytes_accessed=2_000_000, transcendentals=0),
    )(mix_matrix, rows)


def mix_add(tokens, mix_matrix, rows):
    return pl.pallas_call(
        mix_add_kernel,
        out_shape=jax.ShapeDtypeStruct((TOK_DEV, rows.shape[1]), BF16),
        compiler_params=pltpu.CompilerParams(vmem_limit_bytes=MATMUL_VMEM),
        cost_estimate=pl.CostEstimate(flops=2 * TOK_DEV * rows.size, bytes_accessed=2_000_000, transcendentals=0),
    )(tokens, mix_matrix, rows)


def assemble_kernel(at_ref, *refs):
    pieces, out_ref, sems = refs[:-2], refs[-2], refs[-1]
    copies = []
    for i, piece in enumerate(pieces):
        start = pl.multiple_of(at_ref[i] * 256, 256)
        copies.append(pltpu.make_async_copy(piece, out_ref.at[:, pl.ds(start, piece.shape[1])], sems.at[i]))
    for copy in copies:
        copy.start()
    for copy in copies:
        copy.wait()


def assemble(at, pieces):
    return pl.pallas_call(
        assemble_kernel,
        in_specs=[pl.BlockSpec(memory_space=pltpu.SMEM)] + [pl.BlockSpec(memory_space=pl.ANY)] * len(pieces),
        out_specs=pl.BlockSpec(memory_space=pl.ANY),
        out_shape=jax.ShapeDtypeStruct((TOK_DEV, D), BF16),
        scratch_shapes=[pltpu.SemaphoreType.DMA((len(pieces),))],
        compiler_params=pltpu.CompilerParams(vmem_limit_bytes=MATMUL_VMEM),
        cost_estimate=pl.CostEstimate(flops=0, bytes_accessed=3_000_000, transcendentals=0),
    )(at, *pieces)


def swap(values):
    return lax.ppermute(values, "pp", [(0, 1), (1, 0)])


def along_z(values, step):
    count = lax.axis_size("dp")
    return lax.ppermute(values, "dp", [(i, (i + step) % count) for i in range(count)])


def to_experts(rows):
    width = rows.shape[1]
    return lax.all_to_all(rows.reshape(EXPERTS, CAP, width), "ep", split_axis=0, concat_axis=0, tiled=True).reshape(ROWS, width)


def silu(value):
    return 0.5 * value * (1.0 + jnp.tanh(0.5 * value))


def after(earlier, values):
    return lax.optimization_barrier((earlier, values))[1]


def on_device(tokens, norm_gain, router_weight, expert_ids, up_weight, down_weight):
    core = lax.axis_index("pp").astype(jnp.int32)
    z = lax.axis_index("dp").astype(jnp.int32)
    other = 1 - core
    up = up_weight.reshape(2, HALF, up_weight.shape[2])
    down = down_weight[0]

    outgoing, key, gate = route(tokens, norm_gain, router_weight, expert_ids)
    token_wide = lax.dynamic_slice(tokens, (0, core * HALF), (TOK_DEV, WIDE))
    token_thin = lax.dynamic_slice(tokens, (0, core * HALF + WIDE + z * THIN), (TOK_DEV, THIN))
    mine = to_experts(outgoing)
    theirs = swap(mine)
    hidden = silu(product(mine, up[core]) + product(theirs, up[other])).astype(BF16)

    def partial_sums(start, width):
        got = swap(product(hidden, columns(down, other * HALF + start, width)).astype(BF16))
        return (product(hidden, columns(down, core * HALF + start, width)) + got.astype(F32)).astype(BF16)

    def place(step):
        return WIDE + (z + step) % 4 * THIN

    sent = [partial_sums(place(step), THIN) for step in Z_STEPS[:-1]]
    arrived = [along_z(piece, step) for piece, step in zip(sent, Z_STEPS[:-1])]
    wide = partial_sums(0, WIDE)
    kept = partial_sums(place(0), THIN)
    thin_sum = lax.optimization_barrier(kept).astype(F32)
    for piece in arrived:
        thin_sum = thin_sum + piece.astype(F32)
    mix_matrix = mix_matrix_of(*lax.optimization_barrier((wide, key, gate))[1:])
    wide_rows, thin_sum = lax.optimization_barrier((to_experts(wide), thin_sum.astype(BF16)))
    wide_part = mix(mix_matrix, wide_rows)
    thin_own = mix_add(token_thin, mix_matrix, to_experts(thin_sum))

    wide_own = token_wide.astype(F32) + wide_part.astype(F32)
    for step in (3, 1, 2):
        wide_own = wide_own + along_z(wide_part, step).astype(F32)
    wide_own = wide_own.astype(BF16)
    thin_all = [along_z(thin_own, step) for step in TAIL_STEPS[:-1]] + [thin_own]
    pieces = [wide_own, swap(wide_own)] + thin_all + [swap(piece) for piece in thin_all]
    sources = (z - jnp.array(TAIL_STEPS, jnp.int32)) % 4
    places = jnp.concatenate([jnp.stack([core * 6, other * 6]), core * 6 + 2 + sources, other * 6 + 2 + sources])
    return assemble(places.astype(jnp.int32), pieces)


def solution(mesh):
    in_specs = (
        P("ep", None),
        P(),
        P(),
        P("ep", None),
        P("ep", None, ("pp", "dp")),
        P("ep", ("pp", "dp"), None),
    )
    return jax.shard_map(on_device, mesh=mesh, in_specs=in_specs, out_specs=P("ep", None), check_vma=False)
```

```python
import jax
import jax.numpy as jnp
from jax import lax
from jax.experimental import pallas as pl
from jax.experimental.pallas import tpu as pltpu
from jax.sharding import PartitionSpec as P

D = 3072
EXPERTS = 16
TOP = 4
TOK_DEV = 256
CAP = 72
ROWS = EXPERTS * CAP
HALF = D // 2
WIDE = 512
THIN = 256
Z_STEPS = (1, 3, 2, 0)
TAIL_STEPS = (2, 3, 1, 0)
EPSILON = 1e-05
F32 = jnp.float32
BF16 = jnp.bfloat16
ROUTE_VMEM = 60 * 1024 * 1024
MATMUL_VMEM = 6 * 1024 * 1024
ROUTE_BLOCK = 128
PICK = 2
NORM_ROWS = 16
NT = (((1,), (1,)), ((), ()))


def slot_rows(keys):
    slot = lax.broadcasted_iota(jnp.int32, (CAP, TOK_DEV), 0).astype(F32)
    return jnp.concatenate([(slot == keys[e : e + 1, :]).astype(F32) for e in range(keys.shape[0])], axis=0).astype(BF16)


def route_kernel(tok_hbm, gain_hbm, router_hbm, ids_hbm, rows_hbm, key_hbm, gate_hbm, tok_ref, gain_ref, router_ref, ids_ref, normed_ref, rows_ref, key_ref, gate_ref, sems, out_sems):
    small = [
        pltpu.make_async_copy(ids_hbm, ids_ref, sems.at[0]),
        pltpu.make_async_copy(gain_hbm, gain_ref, sems.at[1]),
        pltpu.make_async_copy(router_hbm, router_ref, sems.at[2]),
    ]
    blocks = [pl.ds(begin, ROUTE_BLOCK) for begin in range(0, TOK_DEV, ROUTE_BLOCK)]
    loads = [pltpu.make_async_copy(tok_hbm.at[block], tok_ref.at[block], sems.at[3 + i]) for i, block in enumerate(blocks)]
    for copy in small[:2] + loads + small[2:]:
        copy.start()

    small[0].wait()
    named = jnp.zeros((EXPERTS, TOK_DEV), jnp.int32)
    expert = lax.broadcasted_iota(jnp.int32, (EXPERTS, TOK_DEV), 0)
    for k in range(TOP):
        named += (ids_ref[k : k + 1, :] == expert).astype(jnp.int32)
    named = named.astype(F32)
    row = lax.broadcasted_iota(jnp.int32, (TOK_DEV, TOK_DEV), 0)
    col = lax.broadcasted_iota(jnp.int32, (TOK_DEV, TOK_DEV), 1)
    earlier = (row > col).astype(F32).astype(BF16)
    same = (row == col).astype(F32).astype(BF16)
    named_bf = named.astype(BF16)
    place_t = lax.dot_general(named_bf, earlier, NT, preferred_element_type=F32)
    key_t = jnp.where(named > 0.5, place_t, -1.0)
    place = lax.dot_general(earlier, named_bf, NT, preferred_element_type=F32)
    chosen = lax.dot_general(same, named_bf, NT, preferred_element_type=F32) > 0.5
    key = jnp.where(chosen, place, -1.0)

    def norm_rows(part, carry):
        rows = pl.ds(pl.multiple_of(part * NORM_ROWS, NORM_ROWS), NORM_ROWS)
        values = tok_ref[rows, :].astype(F32)
        shifted = values - jnp.mean(values, axis=-1, keepdims=True)
        spread = jnp.mean(shifted * shifted, axis=-1, keepdims=True)
        normed = (shifted * lax.rsqrt(spread + EPSILON) * gain_ref[...]).astype(BF16)
        normed_ref[0, rows, :] = normed[:, :HALF]
        normed_ref[1, rows, :] = normed[:, HALF:]
        return carry

    small[1].wait()
    turns = ROUTE_BLOCK // NORM_ROWS
    for i, copy in enumerate(loads):
        copy.wait()
        lax.fori_loop(i * turns, (i + 1) * turns, norm_rows, 0, unroll=True)

    core = lax.axis_index("pp")
    stores = []
    for i in range(EXPERTS // PICK):
        rows = pl.ds(i * PICK * CAP, PICK * CAP)
        pick = slot_rows(key_t[i * PICK : (i + 1) * PICK, :])
        rows_ref[rows, :] = jnp.dot(pick, normed_ref[core], preferred_element_type=F32).astype(BF16)
        stores.append(pltpu.make_async_copy(rows_ref.at[rows], rows_hbm.at[rows], out_sems.at[i]))
        stores[-1].start()

    small[2].wait()
    logits = lax.dot_general(normed_ref[0], router_ref[:, :HALF], NT, preferred_element_type=F32)
    logits += lax.dot_general(normed_ref[1], router_ref[:, HALF:], NT, preferred_element_type=F32)
    weight = jnp.where(chosen, jnp.exp(logits), 0.0)
    gate = weight / jnp.sum(weight, axis=1, keepdims=True)
    key_ref[...] = key
    gate_ref[...] = gate
    for i, (here, there) in enumerate(((key_ref, key_hbm), (gate_ref, gate_hbm))):
        stores.append(pltpu.make_async_copy(here, there, out_sems.at[EXPERTS // PICK + i]))
        stores[-1].start()
    for copy in stores:
        copy.wait()


def route(tokens, norm_gain, router_weight, expert_ids):
    shapes = [((ROWS, HALF), BF16), ((TOK_DEV, EXPERTS), F32), ((TOK_DEV, EXPERTS), F32)]
    held = [((TOK_DEV, D), BF16), ((1, D), F32), ((EXPERTS, D), BF16), ((TOP, TOK_DEV), jnp.int32), ((2, TOK_DEV, HALF), BF16)]
    anywhere = pl.BlockSpec(memory_space=pl.ANY)
    return pl.pallas_call(
        route_kernel,
        in_specs=[anywhere] * 4,
        out_specs=[anywhere] * 3,
        out_shape=[jax.ShapeDtypeStruct(shape, kind) for shape, kind in shapes],
        scratch_shapes=[pltpu.VMEM(shape, kind) for shape, kind in held + shapes]
        + [pltpu.SemaphoreType.DMA((3 + TOK_DEV // ROUTE_BLOCK,)), pltpu.SemaphoreType.DMA((EXPERTS // PICK + 2,))],
        compiler_params=pltpu.CompilerParams(vmem_limit_bytes=ROUTE_VMEM),
        cost_estimate=pl.CostEstimate(flops=2 * ROWS * TOK_DEV * HALF, bytes_accessed=6_000_000, transcendentals=0),
    )(tokens, norm_gain.reshape(1, D), router_weight.T, expert_ids.T)


def mix_matrix_kernel(key_ref, gate_ref, mix_ref):
    slot = lax.broadcasted_iota(jnp.int32, (EXPERTS, ROWS), 1)
    first = lax.broadcasted_iota(jnp.int32, (EXPERTS, ROWS), 0) * CAP
    inside = (slot >= first) & (slot < first + CAP)
    spread_out = inside.astype(F32).astype(BF16)
    slot_in = jnp.sum(jnp.where(inside, slot - first, 0).astype(F32), axis=0, keepdims=True)
    key_wide = jnp.dot(key_ref[...].astype(BF16), spread_out, preferred_element_type=F32)
    gate_wide = jnp.dot(gate_ref[...].astype(BF16), spread_out, preferred_element_type=F32)
    mix_ref[...] = jnp.where(key_wide == slot_in, gate_wide, 0.0).astype(BF16)


def mix_matrix_of(key, gate):
    return pl.pallas_call(
        mix_matrix_kernel,
        out_shape=jax.ShapeDtypeStruct((TOK_DEV, ROWS), BF16),
        compiler_params=pltpu.CompilerParams(vmem_limit_bytes=MATMUL_VMEM),
        cost_estimate=pl.CostEstimate(flops=4 * ROWS * TOK_DEV * EXPERTS, bytes_accessed=1_000_000, transcendentals=0),
    )(key, gate)


def product(rows, weight):
    return jnp.dot(rows, weight, preferred_element_type=F32)


def columns(weight, start, width):
    return lax.dynamic_slice_in_dim(weight, start, width, axis=1)


def mix_kernel(mix_ref, rows_ref, out_ref):
    out_ref[...] = jnp.dot(mix_ref[...], rows_ref[...], preferred_element_type=F32).astype(BF16)


def mix_add_kernel(tok_ref, mix_ref, rows_ref, out_ref):
    total = jnp.dot(mix_ref[...], rows_ref[...], preferred_element_type=F32)
    out_ref[...] = (tok_ref[...].astype(F32) + total).astype(BF16)


def mix(mix_matrix, rows):
    return pl.pallas_call(
        mix_kernel,
        out_shape=jax.ShapeDtypeStruct((TOK_DEV, rows.shape[1]), BF16),
        compiler_params=pltpu.CompilerParams(vmem_limit_bytes=MATMUL_VMEM),
        cost_estimate=pl.CostEstimate(flops=2 * TOK_DEV * rows.size, bytes_accessed=2_000_000, transcendentals=0),
    )(mix_matrix, rows)


def mix_add(tokens, mix_matrix, rows):
    return pl.pallas_call(
        mix_add_kernel,
        out_shape=jax.ShapeDtypeStruct((TOK_DEV, rows.shape[1]), BF16),
        compiler_params=pltpu.CompilerParams(vmem_limit_bytes=MATMUL_VMEM),
        cost_estimate=pl.CostEstimate(flops=2 * TOK_DEV * rows.size, bytes_accessed=2_000_000, transcendentals=0),
    )(tokens, mix_matrix, rows)


def assemble_kernel(at_ref, *refs):
    pieces, out_ref, sems = refs[:-2], refs[-2], refs[-1]
    copies = []
    for i, piece in enumerate(pieces):
        start = pl.multiple_of(at_ref[i] * 256, 256)
        copies.append(pltpu.make_async_copy(piece, out_ref.at[:, pl.ds(start, piece.shape[1])], sems.at[i]))
    for copy in copies:
        copy.start()
    for copy in copies:
        copy.wait()


def assemble(at, pieces):
    return pl.pallas_call(
        assemble_kernel,
        in_specs=[pl.BlockSpec(memory_space=pltpu.SMEM)] + [pl.BlockSpec(memory_space=pl.ANY)] * len(pieces),
        out_specs=pl.BlockSpec(memory_space=pl.ANY),
        out_shape=jax.ShapeDtypeStruct((TOK_DEV, D), BF16),
        scratch_shapes=[pltpu.SemaphoreType.DMA((len(pieces),))],
        compiler_params=pltpu.CompilerParams(vmem_limit_bytes=MATMUL_VMEM),
        cost_estimate=pl.CostEstimate(flops=0, bytes_accessed=3_000_000, transcendentals=0),
    )(at, *pieces)


def swap(values):
    return lax.ppermute(values, "pp", [(0, 1), (1, 0)])


def along_z(values, step):
    count = lax.axis_size("dp")
    return lax.ppermute(values, "dp", [(i, (i + step) % count) for i in range(count)])


def to_experts(rows):
    width = rows.shape[1]
    return lax.all_to_all(rows.reshape(EXPERTS, CAP, width), "ep", split_axis=0, concat_axis=0, tiled=True).reshape(ROWS, width)


def silu(value):
    return 0.5 * value * (1.0 + jnp.tanh(0.5 * value))


def after(earlier, values):
    return lax.optimization_barrier((earlier, values))[1]


def on_device(tokens, norm_gain, router_weight, expert_ids, up_weight, down_weight):
    core = lax.axis_index("pp").astype(jnp.int32)
    z = lax.axis_index("dp").astype(jnp.int32)
    other = 1 - core
    up = up_weight.reshape(2, HALF, up_weight.shape[2])
    down = down_weight[0]

    outgoing, key, gate = route(tokens, norm_gain, router_weight, expert_ids)
    token_wide = lax.dynamic_slice(tokens, (0, core * HALF), (TOK_DEV, WIDE))
    token_thin = lax.dynamic_slice(tokens, (0, core * HALF + WIDE + z * THIN), (TOK_DEV, THIN))
    mine = to_experts(outgoing)
    theirs = swap(mine)
    hidden = silu(product(mine, up[core]) + product(theirs, up[other])).astype(BF16)

    def partial_sums(start, width):
        got = swap(product(hidden, columns(down, other * HALF + start, width)).astype(BF16))
        return (product(hidden, columns(down, core * HALF + start, width)) + got.astype(F32)).astype(BF16)

    def place(step):
        return WIDE + (z + step) % 4 * THIN

    sent = [partial_sums(place(step), THIN) for step in Z_STEPS[:-1]]
    arrived = [along_z(piece, step) for piece, step in zip(sent, Z_STEPS[:-1])]
    wide = partial_sums(0, WIDE)
    kept = partial_sums(place(0), THIN)
    thin_sum = lax.optimization_barrier(kept).astype(F32)
    for piece in arrived:
        thin_sum = thin_sum + piece.astype(F32)
    mix_matrix = mix_matrix_of(*lax.optimization_barrier((wide, key, gate))[1:])
    wide_rows, thin_sum = lax.optimization_barrier((to_experts(wide), thin_sum.astype(BF16)))
    wide_part = mix(mix_matrix, wide_rows)
    thin_own = mix_add(token_thin, mix_matrix, to_experts(thin_sum))

    wide_own = token_wide.astype(F32) + wide_part.astype(F32)
    for step in (3, 1, 2):
        wide_own = wide_own + along_z(wide_part, step).astype(F32)
    wide_own = wide_own.astype(BF16)
    thin_all = [along_z(thin_own, step) for step in TAIL_STEPS[:-1]] + [thin_own]
    pieces = [wide_own, swap(wide_own)] + thin_all + [swap(piece) for piece in thin_all]
    sources = (z - jnp.array(TAIL_STEPS, jnp.int32)) % 4
    places = jnp.concatenate([jnp.stack([core * 6, other * 6]), core * 6 + 2 + sources, other * 6 + 2 + sources])
    return assemble(places.astype(jnp.int32), pieces)


def solution(mesh):
    in_specs = (
        P("ep", None),
        P(),
        P(),
        P("ep", None),
        P("ep", None, ("pp", "dp")),
        P("ep", ("pp", "dp"), None),
    )
    return jax.shard_map(on_device, mesh=mesh, in_specs=in_specs, out_specs=P("ep", None), check_vma=False)
```
